32 devices in a mesh: basin: 2 (over y), tx: 4 (over z), ty: 2 (over core), ev: 2 (over x).
Axes of the slice: x: 2, y: 2, z: 4, core: 2. Of those that a mesh axis runs over, the one named last changes fastest.
Arguments:
- depth0: float32 [4, 8, 8, 8, 256], P(('basin', 'ev'), None, None, 'tx', 'ty'), parts along dimension 0, may hold values from 0.6 to 1.4
- momentum0: float32 [4, 2, 8, 8, 8, 256], P(('basin', 'ev'), None, None, None, 'tx', 'ty'), parts along dimension 0, may hold values from -2.5 to 2.5
- obs_weight: float32 [4, 8, 8, 8, 256], P(('basin', 'ev'), None, None, 'tx', 'ty'), parts along dimension 0, as said below
- wet_mask: int32 [4, 4, 8, 256], P(('basin', 'ev'), None, 'tx', 'ty'), parts along dimension 0, may hold values 0 or 1
- zone_id: int32 [16, 256], P(('basin', 'tx'), 'ty'), parts along dimension 0, may hold values from 0 to 31
- manning: float32 [64], P('basin'), parts along dimension 0, may hold values from 0.2 to 0.6
Outputs:
- adjoint_state: float32 [4, 3, 8, 8, 8, 256], P(('basin', 'ev'), None, None, None, 'tx', 'ty'), parts along dimension 0
- rough_grad: float32 [64], P('basin'), parts along dimension 0
The draws below stay inside these ranges and needn't reach their ends.
There are 2 independent parts, one for each index of `basin`. The reference program is written for one: setup_inputs(seed, part) draws one part's arguments, and reference() takes and returns one part's arrays. A program takes and returns all parts, laid end to end along the dimension named above; each array names one. Nothing has to cross between parts.
Inputs may be any that keep to these rules, and one draw needn't show every extreme that they name: `wet_mask`: 1 where an element is wet in that section of that event, else 0. `obs_weight`: positive weights.
All inputs are finite; a program needn't handle non-finite values. No bound on the sum of `wet_mask` on one device may be relied on, other than what follows from the above.
Results may differ from the reference program's by a relative error of at most 0.00005.
Values sent between devices are 32-bit elements; how exact they have to be, the bound alone decides.
A program may use at most 64 MiB of HBM per device.

```python
import math
import jax
import jax.numpy as jnp
import numpy as np
from jax import lax

NP = 8
SECTIONS = 4
ZONES = 32
NEX = 8
NEY = 256
EVENTS = 2


def draw_obs_weight(key, part):
    shape = (EVENTS, NP, NP, NEX, NEY)
    base = jnp.exp(jax.random.uniform(key, shape, jnp.float32, math.log(0.1), math.log(0.3)))
    ramp_event = 1.0 + 2.0 * jnp.arange(EVENTS, dtype=jnp.float32) / max(EVENTS - 1, 1)
    ramp_x = 1.0 + 2.0 * jnp.arange(NEX, dtype=jnp.float32) / max(NEX - 1, 1)
    ramp_y = 1.0 + 2.0 * jnp.arange(NEY, dtype=jnp.float32) / max(NEY - 1, 1)
    return base * ramp_event[:, None, None, None, None] * ramp_x[None, None, None, :, None] * ramp_y[None, None, None, None, :]


def set_ends(array, own_key, least, high):
    extent = array.shape
    spot = [jax.random.randint(jax.random.fold_in(own_key, axis), (), 0, extent[axis]) for axis in range(len(extent))]
    array = array.at[tuple(spot)].set(least)
    longest = extent.index(max(extent))
    spot[longest] = (spot[longest] + 1) % extent[longest]
    return array.at[tuple(spot)].set(high)


def block_scale(key, dims, pieces, least, high):
    def one(dim, parts):
        draws = jax.random.uniform(jax.random.fold_in(jax.random.fold_in(key, 6), dim), (parts,), jnp.float32, least / len(pieces), high / len(pieces))
        return jnp.repeat(jnp.exp(draws), dims[dim] // parts).reshape((-1,) + (1,) * (len(dims) - dim - 1))

    factor_of = one(*pieces[0])
    for cut in pieces[1:]:
        factor_of = factor_of * one(*cut)
    return factor_of


def gaussian(own_key, shape, width, most, shards=(), kind=jnp.bfloat16):
    factor_of = block_scale(own_key, shape, shards, -0.22, 0.18) if shards else 1.0
    values = jax.random.normal(own_key, shape, jnp.float32) * width * factor_of
    return jnp.minimum(jnp.maximum(values, -most), most).astype(kind)


def setup_inputs(seed: int = 0, part: int = 0) -> dict:
    keys = jax.random.split(jax.random.key(seed), 7)
    own_keys = jax.random.split(jax.random.fold_in(keys[6], part), 7)
    depth0 = jnp.clip(0.6 + 0.79999995 * jax.random.uniform(own_keys[0], (EVENTS, NP, NP, NEX, NEY), jnp.float32) ** block_scale(own_keys[0], (EVENTS, NP, NP, NEX, NEY), ((0, 2), (3, 4), (4, 2)), -0.2, 0.2), 0.6, 1.4)
    momentum0 = gaussian(own_keys[1], (EVENTS, 2, NP, NP, NEX, NEY), 0.5, 2.5, ((0, 2), (4, 4), (5, 2)), jnp.float32)
    obs_weight = draw_obs_weight(jax.random.fold_in(jax.random.fold_in(keys[6], part), 71), part)
    wet_mask = set_ends((jax.random.randint(own_keys[3], (EVENTS, SECTIONS, NEX, NEY), 0, 5) < 4).astype(jnp.int32), jax.random.fold_in(own_keys[3], 1), 0, 1)
    zone_id = set_ends(jax.random.randint(own_keys[4], (NEX, NEY), 0, ZONES), jax.random.fold_in(own_keys[4], 1), 0, ZONES - 1).astype(jnp.int32)
    manning = jnp.clip(jnp.exp(jax.random.uniform(own_keys[5], (ZONES,), jnp.float32, math.log(0.2), math.log(0.6))), 0.2, 0.6)
    return {"depth0": depth0, "momentum0": momentum0, "obs_weight": obs_weight, "wet_mask": wet_mask, "zone_id": zone_id, "manning": manning}


GRAVITY = 1.0
PENALTY_SPEED = 4.0
TIME_STEP = 0.0005
SPEED_FLOOR = 0.01

def node_tables():
    points = -np.cos(np.pi * np.arange(NP) / (NP - 1))
    identity = np.eye(NP)
    differ = points[:, None] - points[None, :] + identity
    barycentric = 1.0 / np.prod(differ, axis=1)
    derivative = barycentric[None, :] / barycentric[:, None] / differ * (1.0 - identity)
    derivative = derivative - identity * derivative.sum(axis=1)[:, None]
    order = NP - 1
    if order % 2 == 1:
        end_weight = 1.0 / (order * order)
    else:
        end_weight = 1.0 / (order * order - 1)
    return (derivative, float(1.0 / end_weight))

def fluxes(state, direction):
    depth = state[:, 0]
    flow_x = state[:, 1]
    flow_y = state[:, 2]
    pressure = 0.5 * GRAVITY * depth * depth
    if direction == 0:
        veloc = flow_x / depth
        return jnp.stack([flow_x, flow_x * veloc + pressure, flow_y * veloc], axis=1)
    veloc = flow_y / depth
    return jnp.stack([flow_y, flow_x * veloc, flow_y * veloc + pressure], axis=1)

def face_terms(left_state, right_state, direction, lift_coef):
    flux_left = fluxes(left_state, direction)
    flux_right = fluxes(right_state, direction)
    common = 0.5 * (flux_left + flux_right) - 0.5 * PENALTY_SPEED * (right_state - left_state)
    return (lift_coef * (flux_left - common), lift_coef * (common - flux_right))

def tendency_of(state, neighbours, rough_elem, wet_now, derivative, lift_coef):
    west_nbr, east_nbr, south_nbr, north_nbr = neighbours
    flux_x = fluxes(state, 0)
    flux_y = fluxes(state, 1)
    divergence = jnp.einsum('ai,ecibxy->ecabxy', derivative, flux_x, precision=lax.Precision.HIGHEST)
    divergence = divergence + jnp.einsum('bj,ecajxy->ecabxy', derivative, flux_y, precision=lax.Precision.HIGHEST)
    unused_one, west_term = face_terms(west_nbr, state[:, :, 0], 0, lift_coef)
    east_term, unused_two = face_terms(state[:, :, -1], east_nbr, 0, lift_coef)
    unused_three, south_term = face_terms(south_nbr, state[:, :, :, 0], 1, lift_coef)
    north_term, unused_four = face_terms(state[:, :, :, -1], north_nbr, 1, lift_coef)
    tendency = -divergence
    tendency = tendency.at[:, :, 0].add(west_term)
    tendency = tendency.at[:, :, -1].add(east_term)
    tendency = tendency.at[:, :, :, 0].add(south_term)
    tendency = tendency.at[:, :, :, -1].add(north_term)
    depth = state[:, 0]
    veloc_x = state[:, 1] / depth
    veloc_y = state[:, 2] / depth
    speed_norm = jnp.sqrt(veloc_x * veloc_x + veloc_y * veloc_y + SPEED_FLOOR)
    drag = -GRAVITY * rough_elem * rough_elem * speed_norm / jnp.power(depth, 4.0 / 3.0)
    tendency = tendency.at[:, 1].add(drag * state[:, 1])
    tendency = tendency.at[:, 2].add(drag * state[:, 2])
    return wet_now[:, None, None, None] * tendency

def neighbors(state):
    own_west = state[:, :, 0]
    own_east = state[:, :, -1]
    own_south = state[:, :, :, 0]
    own_north = state[:, :, :, -1]
    west_nbr = jnp.concatenate([own_west[:, :, :, :1], own_east[:, :, :, :-1]], axis=3)
    east_nbr = jnp.concatenate([own_west[:, :, :, 1:], own_east[:, :, :, -1:]], axis=3)
    south_nbr = jnp.concatenate([own_south[:, :, :, :, :1], own_north[:, :, :, :, :-1]], axis=4)
    north_nbr = jnp.concatenate([own_south[:, :, :, :, 1:], own_north[:, :, :, :, -1:]], axis=4)
    return (west_nbr, east_nbr, south_nbr, north_nbr)

def reference(depth0, momentum0, obs_weight, wet_mask, zone_id, manning):
    table, lift_coef = node_tables()
    derivative = jnp.asarray(table, jnp.float32)

    def one_event(inputs):
        depth_event, momentum_event, weight_event, wet_event = inputs
        start = jnp.concatenate([depth_event[None, None], momentum_event[None]], axis=1)

        def forward(start_state, rough):
            rough_elem = rough[zone_id]

            def section_rhs(state, section_index):
                wet_now = wet_event[section_index][None].astype(jnp.float32)
                return tendency_of(state, neighbors(state), rough_elem, wet_now, derivative, lift_coef)
            slope_one = section_rhs(start_state, 0)
            slope_two = section_rhs(start_state + 0.5 * TIME_STEP * slope_one, 1)
            slope_three = section_rhs(start_state + 0.5 * TIME_STEP * slope_two, 2)
            slope_four = section_rhs(start_state + TIME_STEP * slope_three, 3)
            return start_state + TIME_STEP / 6.0 * (slope_one + 2.0 * slope_two + 2.0 * slope_three + slope_four)
        final, pullback = jax.vjp(forward, start, manning)
        adjoint_final = jnp.stack([jnp.zeros_like(final[:, 0]), weight_event[None] * final[:, 1], weight_event[None] * final[:, 2]], axis=1)
        adjoint_start, rough_cot = pullback(adjoint_final)
        return (adjoint_start[0], rough_cot)
    adjoint_state, rough_cots = lax.map(one_event, (depth0, momentum0, obs_weight, wet_mask))
    scale = ZONES / (TIME_STEP * EVENTS * NEX * NEY * NP * NP)
    return (adjoint_state, lax.optimization_barrier(jnp.sum(rough_cots, axis=0)) * scale)
```

```python
import functools

import jax
import jax.numpy as jnp
import numpy as np
from jax import lax
from jax.experimental import pallas as pl
from jax.experimental.pallas import tpu as pltpu
from jax.sharding import PartitionSpec as P

NP = 8
SECTIONS = 4
ZONES = 32
SUB = 8

PENALTY_SPEED = 4.0
TIME_STEP = 0.0005
SPEED_FLOOR = 0.01
MESH = pl.DeviceIdType.MESH
EAST, WEST, NORTH, SOUTH = range(4)


def node_tables():
    points = -np.cos(np.pi * np.arange(NP) / (NP - 1))
    identity = np.eye(NP)
    differ = points[:, None] - points[None, :] + identity
    barycentric = 1.0 / np.prod(differ, axis=1)
    derivative = barycentric[None, :] / barycentric[:, None] / differ * (1.0 - identity)
    derivative = derivative - identity * derivative.sum(axis=1)[:, None]
    order = NP - 1
    end_weight = 1.0 / (order * order)
    return (derivative, float(1.0 / end_weight))


def along_first(table, slabs):
    half = NP // 2
    even = [slabs[k] + slabs[NP - 1 - k] for k in range(half)]
    odd = [slabs[k] - slabs[NP - 1 - k] for k in range(half)]
    out = [None] * NP
    for a in range(half):
        on_even = sum(float(0.5 * (table[a, k] + table[a, NP - 1 - k])) * even[k] for k in range(half))
        on_odd = sum(float(0.5 * (table[a, k] - table[a, NP - 1 - k])) * odd[k] for k in range(half))
        out[a] = on_odd + on_even
        out[NP - 1 - a] = on_odd - on_even
    return out


def kernel(
    axes, ext_x, events,
    depth_ref, mom_ref, weight_ref, wet_ref, zone_ref, manning_ref,
    adj_ref, grad_ref,
    state, vel_x, vel_y, inv_h, drag_r, flux_x, flux_y, tend, acc, final_adj, later,
    wet_rows, rough_rows, coef_y, zone_acc,
    xs, xr, ys, yr, zs, zr, send_sem, recv_sem, zsend_sem, zrecv_sem,
):
    table, lift = node_tables()
    n_tx, n_ty, n_ev = axes["tx"], axes["ty"], axes["ev"]
    tx, ty, ev = lax.axis_index("tx"), lax.axis_index("ty"), lax.axis_index("ev")
    ext_y = depth_ref.shape[-1]
    groups = ext_x
    step = ext_x
    has = {EAST: tx < n_tx - 1, WEST: tx > 0, NORTH: ty < n_ty - 1, SOUTH: ty > 0}
    target = {EAST: {"tx": tx + 1}, WEST: {"tx": tx - 1}, NORTH: {"ty": ty + 1}, SOUTH: {"ty": ty - 1}}
    opposite = {EAST: WEST, WEST: EAST, NORTH: SOUTH, SOUTH: NORTH}

    plane = n_ty * n_ev
    here = ty * n_ev + ev
    barrier = pltpu.get_barrier_semaphore()
    plane_peers = []
    for k in range(1, plane):
        other = lax.rem(here + k, plane)
        plane_peers.append((k, {"ty": other // n_ev, "ev": lax.rem(other, n_ev)}))
    line_peers = [(k, {"tx": lax.rem(tx + k, n_tx)}) for k in range(1, n_tx)]
    for _, peer in plane_peers + line_peers:
        pl.semaphore_signal(barrier, inc=1, device_id=peer, device_id_type=MESH)

    sub = lax.broadcasted_iota(jnp.int32, (SUB, ext_y), 0)
    lane = lax.broadcasted_iota(jnp.int32, (SUB, ext_y), 1)
    elem = lax.rem(sub, ext_x)
    one = jnp.float32(1.0)

    def flag(yes):
        return jnp.where(yes, 1, 0)

    inside = {
        WEST: jnp.where((elem == 0) & (flag(has[WEST]) == 0), 0.0, one),
        EAST: jnp.where((elem == ext_x - 1) & (flag(has[EAST]) == 0), 0.0, one),
        SOUTH: jnp.where((sub >= ext_x) | ((lane == 0) & (flag(has[SOUTH]) == 0)), 0.0, one),
        NORTH: jnp.where((sub < SUB - ext_x) | ((lane == ext_y - 1) & (flag(has[NORTH]) == 0)), 0.0, one),
    }
    first_elem = (elem == 0) & (flag(has[WEST]) == 1)
    last_elem = (elem == ext_x - 1) & (flag(has[EAST]) == 1)
    first_lane = (lane == 0) & (flag(has[SOUTH]) == 1)
    last_lane = (lane == ext_y - 1) & (flag(has[NORTH]) == 1)

    def spread(rows):
        out = jnp.broadcast_to(rows[0:1], (SUB, ext_y))
        for e in range(1, ext_x):
            out = jnp.where(elem == e, jnp.broadcast_to(rows[e:e + 1], (SUB, ext_y)), out)
        return out

    for s in range(SECTIONS):
        wet_rows[s] = spread(wet_ref[s].astype(jnp.float32))
    zone = spread(zone_ref[...])
    rough = jnp.zeros((SUB, ext_y), jnp.float32)
    for z in range(ZONES):
        rough = jnp.where(zone == z, manning_ref[z], rough)
    rough_rows[...] = rough

    for t, mat in enumerate((table, table.T)):
        for g in range(groups):
            for h in range(groups):
                for k in range(SUB // step):
                    column = jnp.zeros((SUB, ext_y), jnp.float32)
                    for r in range(SUB):
                        a = (SUB * g + r) // ext_x
                        b = (SUB * h + (r - k * step) % SUB) // ext_x
                        column = jnp.where(sub == r, jnp.float32(-mat[a, b]), column)
                    coef_y[t, g, h, k] = column
    zone_acc[...] = jnp.zeros((SUB, ext_y), jnp.float32)

    def rows(g):
        return pl.ds(SUB * g, SUB)

    def roll(value, shift, axis):
        size = value.shape[axis]
        shift = shift % size
        return value if shift == 0 else pltpu.roll(value, shift, axis)

    def minus_along_second(t, source):
        turned = [[roll(source[h], k * step, 0) for k in range(SUB // step)] for h in range(groups)]
        return [
            sum(coef_y[t, g, h, k] * turned[h][k] for h in range(groups) for k in range(SUB // step))
            for g in range(groups)
        ]

    def copy(rnd, side):
        pair, slot = ((xs, xr), side) if side in (EAST, WEST) else ((ys, yr), side - 2)
        return pltpu.make_async_remote_copy(
            src_ref=pair[0].at[rnd, slot],
            dst_ref=pair[1].at[rnd, slot],
            send_sem=send_sem.at[rnd, side],
            recv_sem=recv_sem.at[rnd, side],
            device_id=target[side],
            device_id_type=MESH,
        )

    def start(rnd, sides):
        for side in sides:
            @pl.when(has[side])
            def _():
                copy(rnd, side).start()

    def await_all(rnd, sides):
        for side in sides:
            @pl.when(has[opposite[side]])
            def _():
                copy(rnd, side).wait_recv()

    def pack_x(rnd, c, east, west):
        to_east, to_west = east[0], west[0]
        for g in range(1, groups):
            to_east = jnp.where(elem == ext_x - 1 - g, roll(east[g], -g, 0), to_east)
            to_west = jnp.where(elem == g, roll(west[g], g, 0), to_west)
        xs[rnd, EAST, c] = to_east
        xs[rnd, WEST, c] = to_west

    def beside_x(rnd, c, g, east, west):
        from_west, from_east = xr[rnd, EAST, c], xr[rnd, WEST, c]
        at_west = jnp.where(first_elem, roll(from_west, -(ext_x - 1 - g), 0), roll(east[g], 1, 0))
        at_east = jnp.where(last_elem, roll(from_east, ext_x - 1 - g, 0), roll(west[g], -1, 0))
        return at_west, at_east

    def pack_y(rnd, c, i, north, south):
        ys[rnd, 0, c, i] = roll(roll(north, ext_x, 0), 1, 1)
        ys[rnd, 1, c, i] = roll(roll(south, -ext_x, 0), -1, 1)

    def beside_y(rnd, c, i):
        at_south = jnp.where(first_lane, yr[rnd, 0, c, i], ys[rnd, 0, c, i])
        at_north = jnp.where(last_lane, yr[rnd, 1, c, i], ys[rnd, 1, c, i])
        return at_south, at_north

    first, last = 0, groups - 1
    comps = range(3)
    pen = 0.5 * PENALTY_SPEED

    def put_fluxes(s, i):
        for g in range(groups):
            h, p, m = (state[s, c, i, rows(g)] for c in comps)
            ih = 1.0 / h
            u, v = p * ih, m * ih
            inv_h[s, i, rows(g)] = ih
            vel_x[s, i, rows(g)] = u
            vel_y[s, i, rows(g)] = v
            pressure = 0.5 * h * h
            cross = p * v
            fx = (p, p * u + pressure, cross)
            fy = (m, cross, m * v + pressure)
            for c, q in enumerate((h, p, m)):
                flux_x[c, i, rows(g)] = fx[c]
                flux_y[c, i, rows(g)] = fy[c]
            if g == last:
                for c, q in enumerate((h, p, m)):
                    ys[s, 0, c, i] = roll(roll(0.5 * fy[c] + pen * q, ext_x, 0), 1, 1)
            if g == first:
                for c, q in enumerate((h, p, m)):
                    ys[s, 1, c, i] = roll(roll(pen * q - 0.5 * fy[c], -ext_x, 0), -1, 1)

    def x_traces(s, c):
        east = [0.5 * flux_x[c, NP - 1, rows(g)] + pen * state[s, c, NP - 1, rows(g)] for g in range(groups)]
        west = [pen * state[s, c, 0, rows(g)] - 0.5 * flux_x[c, 0, rows(g)] for g in range(groups)]
        return east, west

    coefs = (0.5 * TIME_STEP, 0.5 * TIME_STEP, TIME_STEP)
    sums = (1.0, 2.0, 2.0, 1.0)
    final_weights = (TIME_STEP / 6.0, TIME_STEP / 3.0, TIME_STEP / 3.0, TIME_STEP / 6.0)

    def send_forward(s):
        for c in comps:
            pack_x(s, c, *x_traces(s, c))
        start(s, (EAST, WEST, NORTH, SOUTH))

    def set_up(i, _):
        state[0, 0, i] = depth_ref[i]
        state[0, 1, i] = mom_ref[0, i]
        state[0, 2, i] = mom_ref[1, i]
        put_fluxes(0, i)
        return _

    lax.fori_loop(0, NP, set_up, 0)
    pl.semaphore_wait(barrier, len(plane_peers) + len(line_peers))
    send_forward(0)

    for s in range(SECTIONS):
        def volume(i, _):
            for c in comps:
                out = minus_along_second(0, [flux_y[c, i, rows(g)] for g in range(groups)])
                for g in range(groups):
                    tend[c, i, rows(g)] = out[g]
            for g in range(groups):
                h, p, m = (state[s, c, i, rows(g)] for c in comps)
                u, v = vel_x[s, i, rows(g)], vel_y[s, i, rows(g)]
                speed = jnp.sqrt(u * u + v * v + SPEED_FLOOR)
                rough_g = rough_rows[...]
                kr = rough_g * speed * jnp.exp((-4.0 / 3.0) * jnp.log(h))
                drag_r[s, i, rows(g)] = kr
                k = rough_g * kr
                tend[1, i, rows(g)] -= k * p
                tend[2, i, rows(g)] -= k * m
            return _

        lax.fori_loop(0, NP, volume, 0)

        def volume_x(c, _):
            for g in range(groups):
                out = along_first(table, [flux_x[c, i, rows(g)] for i in range(NP)])
                for i in range(NP):
                    tend[c, i, rows(g)] -= out[i]
            return _

        lax.fori_loop(0, 3, volume_x, 0)

        await_all(s, (EAST, WEST, NORTH, SOUTH))
        for c in comps:
            east, west = x_traces(s, c)
            for g in range(groups):
                at_west, at_east = beside_x(s, c, g, east, west)
                q0, q7 = state[s, c, 0, rows(g)], state[s, c, NP - 1, rows(g)]
                f0, f7 = flux_x[c, 0, rows(g)], flux_x[c, NP - 1, rows(g)]
                tend[c, 0, rows(g)] += (lift * inside[WEST]) * (at_west - (0.5 * f0 + pen * q0))
                tend[c, NP - 1, rows(g)] += (lift * inside[EAST]) * (at_east - (pen * q7 - 0.5 * f7))

        def finish(i, _):
            wet = wet_rows[s]
            for c in comps:
                at_south, at_north = beside_y(s, c, i)
                own_s = 0.5 * flux_y[c, i, rows(first)] + pen * state[s, c, i, rows(first)]
                own_n = pen * state[s, c, i, rows(last)] - 0.5 * flux_y[c, i, rows(last)]
                for g in range(groups):
                    slope = tend[c, i, rows(g)]
                    if g == first:
                        slope = slope + (lift * inside[SOUTH]) * (at_south - own_s)
                    if g == last:
                        slope = slope + (lift * inside[NORTH]) * (at_north - own_n)
                    slope = wet * slope
                    start_q = state[0, c, i, rows(g)]
                    if s == 0:
                        acc[c, i, rows(g)] = slope
                    elif s < SECTIONS - 1:
                        acc[c, i, rows(g)] += sums[s] * slope
                    if s < SECTIONS - 1:
                        state[s + 1, c, i, rows(g)] = start_q + coefs[s] * slope
                    elif c > 0:
                        total = acc[c, i, rows(g)] + slope
                        final = start_q + (TIME_STEP / 6.0) * total
                        seed = weight_ref[i, rows(g)] * final
                        final_adj[c - 1, i, rows(g)] = seed
                        adj_ref[c, i, rows(g)] = seed
                    else:
                        adj_ref[c, i, rows(g)] = jnp.zeros((SUB, ext_y), jnp.float32)
            if s < SECTIONS - 1:
                put_fluxes(s + 1, i)
            else:
                put_cot(s, i)
            return _

        def put_cot(s, i):
            wet = wet_rows[s]
            for c in comps:
                cot = []
                for g in range(groups):
                    value = None
                    if c > 0:
                        value = final_weights[s] * final_adj[c - 1, i, rows(g)]
                    if s < SECTIONS - 1:
                        back = coefs[s] * later[c, i, rows(g)]
                        value = back if value is None else value + back
                    if value is None:
                        value = jnp.zeros((SUB, ext_y), jnp.float32)
                    value = wet * value
                    acc[c, i, rows(g)] = value
                    cot.append(value)
                pack_y(2 * SECTIONS - 1 - s, c, i, cot[last], cot[first])

        lax.fori_loop(0, NP, finish, 0)
        if s < SECTIONS - 1:
            send_forward(s + 1)

    def cot_faces(c):
        return (
            [acc[c, NP - 1, rows(g)] for g in range(groups)],
            [acc[c, 0, rows(g)] for g in range(groups)],
        )

    def plane_copy(k, peer):
        return pltpu.make_async_remote_copy(
            src_ref=zs.at[0], dst_ref=zr.at[k],
            send_sem=zsend_sem.at[k], recv_sem=zrecv_sem.at[k],
            device_id=peer, device_id_type=MESH,
        )

    def line_copy(k, peer):
        slot = plane + k
        return pltpu.make_async_remote_copy(
            src_ref=zs.at[1], dst_ref=zr.at[slot],
            send_sem=zsend_sem.at[slot], recv_sem=zrecv_sem.at[slot],
            device_id=peer, device_id_type=MESH,
        )

    for s in reversed(range(SECTIONS)):
        rnd = 2 * SECTIONS - 1 - s
        for c in comps:
            pack_x(rnd, c, *cot_faces(c))
        start(rnd, (EAST, WEST, NORTH, SOUTH))

        def drag_back(i, _):
            for g in range(groups):
                h, p, m = (state[s, c, i, rows(g)] for c in comps)
                u, v, ih = vel_x[s, i, rows(g)], vel_y[s, i, rows(g)], inv_h[s, i, rows(g)]
                kr = drag_r[s, i, rows(g)]
                c1, c2 = acc[1, i, rows(g)], acc[2, i, rows(g)]
                rough_g = rough_rows[...]
                dot = c1 * p + c2 * m
                part = kr * dot
                zone_acc[...] += part
                k = rough_g * kr
                e = rough_g * part * ih
                square = u * u + v * v
                q = 1.0 / (square + SPEED_FLOOR)
                eq = e * q
                tend[0, i, rows(g)] = (4.0 / 3.0) * e + eq * square
                tend[1, i, rows(g)] = -(k * c1 + eq * u)
                tend[2, i, rows(g)] = -(k * c2 + eq * v)
            return _

        lax.fori_loop(0, NP, drag_back, 0)

        if s == 0:
            total = zone_acc[...]
            shift = ext_x
            while shift < SUB:
                total = total + roll(total, shift, 0)
                shift *= 2
            total = -2.0 * total
            zones = lax.broadcasted_iota(jnp.int32, (ZONES, ext_y), 0)
            spot = jnp.zeros((ZONES, ext_y), jnp.float32)
            for e in range(ext_x):
                ids = jnp.broadcast_to(zone_ref[e:e + 1, :], (ZONES, ext_y))
                spot = spot + jnp.where(ids == zones, jnp.broadcast_to(total[e:e + 1], (ZONES, ext_y)), 0.0)
            per_zone = jnp.sum(spot, axis=1, keepdims=True)
            spots = lax.broadcasted_iota(jnp.int32, (ZONES, ext_y), 1)
            line = jnp.sum(jnp.where(zones == spots, jnp.broadcast_to(per_zone, (ZONES, ext_y)), 0.0), axis=0, keepdims=True)
            zs[0] = line
            for k, peer in plane_peers:
                plane_copy(k, peer).start()

        def volume_y(i, _):
            for c in comps:
                out = minus_along_second(1, [acc[c, i, rows(g)] for g in range(groups)])
                for g in range(groups):
                    flux_y[c, i, rows(g)] = out[g]
            return _

        lax.fori_loop(0, NP, volume_y, 0)

        def volume_back(c, _):
            for g in range(groups):
                out = along_first(-table.T, [acc[c, i, rows(g)] for i in range(NP)])
                for i in range(NP):
                    flux_x[c, i, rows(g)] = out[i]
            return _

        lax.fori_loop(0, 3, volume_back, 0)

        await_all(rnd, (EAST, WEST, NORTH, SOUTH))
        if s == 0:
            mine = zs[0]
            for k, peer in plane_peers:
                plane_copy(k, peer).wait_recv()
                mine = mine + zr[k]
            zs[1] = mine
            for k, peer in line_peers:
                line_copy(k, peer).start()
        for c in comps:
            east, west = cot_faces(c)
            for g in range(groups):
                at_west, at_east = beside_x(rnd, c, g, east, west)
                w_in, e_in = lift * inside[WEST], lift * inside[EAST]
                flux_x[c, 0, rows(g)] -= (0.5 * w_in) * (west[g] + at_west)
                tend[c, 0, rows(g)] += (pen * w_in) * (at_west - west[g])
                flux_x[c, NP - 1, rows(g)] += (0.5 * e_in) * (east[g] + at_east)
                tend[c, NP - 1, rows(g)] += (pen * e_in) * (at_east - east[g])

        def finish_back(i, _):
            s_in, n_in = lift * inside[SOUTH], lift * inside[NORTH]
            beside = [beside_y(rnd, c, i) for c in comps]
            for g in range(groups):
                a = [flux_x[c, i, rows(g)] for c in comps]
                b = [flux_y[c, i, rows(g)] for c in comps]
                out = [tend[c, i, rows(g)] for c in comps]
                own = [acc[c, i, rows(g)] for c in comps]
                for c in comps:
                    at_south, at_north = beside[c]
                    if g == first:
                        b[c] = b[c] - (0.5 * s_in) * (own[c] + at_south)
                        out[c] = out[c] + (pen * s_in) * (at_south - own[c])
                    if g == last:
                        b[c] = b[c] + (0.5 * n_in) * (own[c] + at_north)
                        out[c] = out[c] + (pen * n_in) * (at_north - own[c])
                h = state[s, 0, i, rows(g)]
                u, v = vel_x[s, i, rows(g)], vel_y[s, i, rows(g)]
                cross = a[2] + b[1]
                au, bv = a[1] * u, b[2] * v
                cot = (
                    out[0] + (a[1] + b[2]) * h - au * u - bv * v - cross * (u * v),
                    out[1] + a[0] + 2.0 * au + cross * v,
                    out[2] + b[0] + 2.0 * bv + cross * u,
                )
                for c in comps:
                    adj_ref[c, i, rows(g)] += cot[c]
                    if s > 0:
                        later[c, i, rows(g)] = cot[c]
            if s > 0:
                put_cot(s - 1, i)
            return _

        lax.fori_loop(0, NP, finish_back, 0)

    whole = zs[1]
    for k, peer in line_peers:
        line_copy(k, peer).wait_recv()
        whole = whole + zr[plane + k]
    nodes = events * n_ev * ext_x * n_tx * ext_y * n_ty * NP * NP
    grad_ref[...] = whole[:, :ZONES] * (ZONES / (TIME_STEP * nodes))

    for rnd in range(2 * SECTIONS):
        for side in (EAST, WEST, NORTH, SOUTH):
            @pl.when(has[side])
            def _():
                copy(rnd, side).wait_send()
    for k, peer in plane_peers:
        plane_copy(k, peer).wait_send()
    for k, peer in line_peers:
        line_copy(k, peer).wait_send()


def local(axes, depth0, momentum0, obs_weight, wet_mask, zone_id, manning):
    ext_x, ext_y = depth0.shape[3:]
    rows = NP * ext_x
    field = (NP, rows, ext_y)
    rounds = 2 * SECTIONS
    slots = axes["ty"] * axes["ev"] + axes["tx"]
    f32 = jnp.float32
    vmem = pl.BlockSpec(memory_space=pltpu.VMEM)
    adjoint, grad = pl.pallas_call(
        functools.partial(kernel, axes, ext_x, depth0.shape[0]),
        out_shape=(
            jax.ShapeDtypeStruct((3,) + field, f32),
            jax.ShapeDtypeStruct((1, ZONES), f32),
        ),
        in_specs=[vmem] * 5 + [pl.BlockSpec(memory_space=pltpu.SMEM)],
        out_specs=(vmem, vmem),
        scratch_shapes=[
            pltpu.VMEM((SECTIONS, 3) + field, f32),
            pltpu.VMEM((SECTIONS,) + field, f32),
            pltpu.VMEM((SECTIONS,) + field, f32),
            pltpu.VMEM((SECTIONS,) + field, f32),
            pltpu.VMEM((SECTIONS,) + field, f32),
            pltpu.VMEM((3,) + field, f32),
            pltpu.VMEM((3,) + field, f32),
            pltpu.VMEM((3,) + field, f32),
            pltpu.VMEM((3,) + field, f32),
            pltpu.VMEM((2,) + field, f32),
            pltpu.VMEM((3,) + field, f32),
            pltpu.VMEM((SECTIONS, SUB, ext_y), f32),
            pltpu.VMEM((SUB, ext_y), f32),
            pltpu.VMEM((2, ext_x, ext_x, SUB // ext_x, SUB, ext_y), f32),
            pltpu.VMEM((SUB, ext_y), f32),
            pltpu.VMEM((rounds, 2, 3, SUB, ext_y), f32),
            pltpu.VMEM((rounds, 2, 3, SUB, ext_y), f32),
            pltpu.VMEM((rounds, 2, 3, NP, SUB, ext_y), f32),
            pltpu.VMEM((rounds, 2, 3, NP, SUB, ext_y), f32),
            pltpu.VMEM((2, 1, ext_y), f32),
            pltpu.VMEM((slots, 1, ext_y), f32),
            pltpu.SemaphoreType.DMA((rounds, 4)),
            pltpu.SemaphoreType.DMA((rounds, 4)),
            pltpu.SemaphoreType.DMA((slots,)),
            pltpu.SemaphoreType.DMA((slots,)),
        ],
        compiler_params=pltpu.CompilerParams(
            collective_id=0, has_side_effects=True, vmem_limit_bytes=32 * 1024 * 1024
        ),
    )(
        depth0.reshape(field),
        momentum0.reshape((2,) + field),
        obs_weight.reshape(field),
        wet_mask.reshape(wet_mask.shape[1:]),
        zone_id,
        manning,
    )
    return adjoint.reshape((1, 3, NP, NP, ext_x, ext_y)), grad.reshape((ZONES,))


def solution(mesh):
    in_specs = (
        P(("basin", "ev"), None, None, "tx", "ty"),
        P(("basin", "ev"), None, None, None, "tx", "ty"),
        P(("basin", "ev"), None, None, "tx", "ty"),
        P(("basin", "ev"), None, "tx", "ty"),
        P(("basin", "tx"), "ty"),
        P("basin"),
    )
    out_specs = (P(("basin", "ev"), None, None, None, "tx", "ty"), P("basin"))
    return jax.shard_map(
        functools.partial(local, dict(mesh.shape)),
        mesh=mesh, in_specs=in_specs, out_specs=out_specs, check_vma=False,
    )
```

```python
import functools

import jax
import jax.numpy as jnp
import numpy as np
from jax import lax
from jax.experimental import pallas as pl
from jax.experimental.pallas import tpu as pltpu
from jax.sharding import PartitionSpec as P

NP = 8
SECTIONS = 4
ZONES = 32
SUB = 8

PENALTY_SPEED = 4.0
TIME_STEP = 0.0005
SPEED_FLOOR = 0.01
MESH = pl.DeviceIdType.MESH
EAST, WEST, NORTH, SOUTH = range(4)


def node_tables():
    points = -np.cos(np.pi * np.arange(NP) / (NP - 1))
    identity = np.eye(NP)
    differ = points[:, None] - points[None, :] + identity
    barycentric = 1.0 / np.prod(differ, axis=1)
    derivative = barycentric[None, :] / barycentric[:, None] / differ * (1.0 - identity)
    derivative = derivative - identity * derivative.sum(axis=1)[:, None]
    order = NP - 1
    end_weight = 1.0 / (order * order)
    return (derivative, float(1.0 / end_weight))


def along_first(table, slabs):
    half = NP // 2
    even = [slabs[k] + slabs[NP - 1 - k] for k in range(half)]
    odd = [slabs[k] - slabs[NP - 1 - k] for k in range(half)]
    out = [None] * NP
    for a in range(half):
        on_even = sum(float(0.5 * (table[a, k] + table[a, NP - 1 - k])) * even[k] for k in range(half))
        on_odd = sum(float(0.5 * (table[a, k] - table[a, NP - 1 - k])) * odd[k] for k in range(half))
        out[a] = on_odd + on_even
        out[NP - 1 - a] = on_odd - on_even
    return out


def kernel(
    axes, ext_x, events,
    depth_hbm, mom_hbm, weight_hbm, wet_hbm, zone_hbm, manning_hbm,
    adj_ref, grad_ref,
    mom_ref, weight_ref, wet_ref, zone_ref, manning_ref, in_sem,
    state, vel_x, vel_y, inv_h, drag_r, flux_x, flux_y, tend, acc, final_adj, later,
    wet_rows, rough_rows, coef_y, zone_acc,
    xs, xr, ys, yr, zs, zr, send_sem, recv_sem, zsend_sem, zrecv_sem,
):
    table, lift = node_tables()
    n_tx, n_ty, n_ev = axes["tx"], axes["ty"], axes["ev"]
    tx, ty, ev = lax.axis_index("tx"), lax.axis_index("ty"), lax.axis_index("ev")
    ext_y = depth_hbm.shape[-1]
    groups = ext_x
    step = ext_x
    per = SUB // ext_x
    blocks = NP // per
    has = {EAST: tx < n_tx - 1, WEST: tx > 0, NORTH: ty < n_ty - 1, SOUTH: ty > 0}
    target = {EAST: {"tx": tx + 1}, WEST: {"tx": tx - 1}, NORTH: {"ty": ty + 1}, SOUTH: {"ty": ty - 1}}
    opposite = {EAST: WEST, WEST: EAST, NORTH: SOUTH, SOUTH: NORTH}

    arrive = [
        pltpu.make_async_copy(source, target_ref, in_sem.at[n])
        for n, (source, target_ref) in enumerate((
            (zone_hbm, zone_ref), (manning_hbm, manning_ref), (wet_hbm, wet_ref),
            (depth_hbm, state.at[0, 0]), (mom_hbm, mom_ref), (weight_hbm, weight_ref),
        ))
    ]
    for piece in arrive:
        piece.start()

    plane = n_ty * n_ev
    here = ty * n_ev + ev
    barrier = pltpu.get_barrier_semaphore()
    plane_peers = []
    for k in range(1, plane):
        other = lax.rem(here + k, plane)
        plane_peers.append((k, {"ty": other // n_ev, "ev": lax.rem(other, n_ev)}))
    line_peers = [(k, {"tx": lax.rem(tx + k, n_tx)}) for k in range(1, n_tx)]
    for _, peer in plane_peers + line_peers:
        pl.semaphore_signal(barrier, inc=1, device_id=peer, device_id_type=MESH)

    sub = lax.broadcasted_iota(jnp.int32, (SUB, ext_y), 0)
    lane = lax.broadcasted_iota(jnp.int32, (SUB, ext_y), 1)
    elem = lax.rem(sub, ext_x)

    def flag(yes):
        return jnp.where(yes, 1, 0)

    zero = jnp.float32(0.0)
    inside = {
        WEST: jnp.where((elem == 0) & (flag(has[WEST]) == 0), zero, lift),
        EAST: jnp.where((elem == ext_x - 1) & (flag(has[EAST]) == 0), zero, lift),
        SOUTH: jnp.where((sub >= ext_x) | ((lane == 0) & (flag(has[SOUTH]) == 0)), zero, lift),
        NORTH: jnp.where((sub < SUB - ext_x) | ((lane == ext_y - 1) & (flag(has[NORTH]) == 0)), zero, lift),
    }
    first_elem = (elem == 0) & (flag(has[WEST]) == 1)
    last_elem = (elem == ext_x - 1) & (flag(has[EAST]) == 1)
    first_lane = (lane == 0) & (flag(has[SOUTH]) == 1)
    last_lane = (lane == ext_y - 1) & (flag(has[NORTH]) == 1)

    def spread(rows):
        out = jnp.broadcast_to(rows[0:1], (SUB, ext_y))
        for e in range(1, ext_x):
            out = jnp.where(elem == e, jnp.broadcast_to(rows[e:e + 1], (SUB, ext_y)), out)
        return out

    for t, mat in enumerate((table, table.T)):
        for g in range(groups):
            for h in range(groups):
                for k in range(SUB // step):
                    column = jnp.zeros((SUB, ext_y), jnp.float32)
                    for r in range(SUB):
                        a = (SUB * g + r) // ext_x
                        b = (SUB * h + (r - k * step) % SUB) // ext_x
                        column = jnp.where(sub == r, jnp.float32(-mat[a, b]), column)
                    coef_y[t, g, h, k] = column
    for piece in arrive[:3]:
        piece.wait()
    for s in range(SECTIONS):
        wet_rows[s] = spread(wet_ref[s].astype(jnp.float32))
    zone = spread(zone_ref[...])
    rough = jnp.zeros((SUB, ext_y), jnp.float32)
    for z in range(ZONES):
        rough = jnp.where(zone == z, manning_ref[z], rough)
    rough_rows[...] = rough

    zone_acc[...] = jnp.zeros((SUB, ext_y), jnp.float32)

    def rows(g):
        return pl.ds(SUB * g, SUB)

    def roll(value, shift, axis):
        size = value.shape[axis]
        shift = shift % size
        return value if shift == 0 else pltpu.roll(value, shift, axis)

    def load_coef(t):
        return [[[coef_y[t, g, h, k] for k in range(per)] for h in range(groups)] for g in range(groups)]

    def minus_along_second(coef, source):
        turned = [[roll(source[h], k * step, 0) for k in range(per)] for h in range(groups)]
        return [
            sum(coef[g][h][k] * turned[h][k] for h in range(groups) for k in range(per))
            for g in range(groups)
        ]

    def copy(rnd, side):
        pair, slot = ((xs, xr), side) if side in (EAST, WEST) else ((ys, yr), side - 2)
        return pltpu.make_async_remote_copy(
            src_ref=pair[0].at[rnd, slot],
            dst_ref=pair[1].at[rnd, slot],
            send_sem=send_sem.at[rnd, side],
            recv_sem=recv_sem.at[rnd, side],
            device_id=target[side],
            device_id_type=MESH,
        )

    def start(rnd, sides):
        for side in sides:
            @pl.when(has[side])
            def _():
                copy(rnd, side).start()

    def await_all(rnd, sides):
        for side in sides:
            @pl.when(has[opposite[side]])
            def _():
                copy(rnd, side).wait_recv()

    def pack_x(rnd, c, east, west):
        to_east, to_west = east[0], west[0]
        for g in range(1, groups):
            to_east = jnp.where(elem == ext_x - 1 - g, roll(east[g], -g, 0), to_east)
            to_west = jnp.where(elem == g, roll(west[g], g, 0), to_west)
        xs[rnd, EAST, c] = to_east
        xs[rnd, WEST, c] = to_west

    def beside_x(rnd, c, g, east, west):
        from_west, from_east = xr[rnd, EAST, c], xr[rnd, WEST, c]
        at_west = jnp.where(first_elem, roll(from_west, -(ext_x - 1 - g), 0), roll(east[g], 1, 0))
        at_east = jnp.where(last_elem, roll(from_east, ext_x - 1 - g, 0), roll(west[g], -1, 0))
        return at_west, at_east

    slot_of = sub // ext_x

    def pack_y(rnd, c, blk, north, south):
        to_north, to_south = roll(north[0], ext_x, 0), south[0]
        for k in range(1, per):
            to_north = jnp.where(slot_of == k, roll(north[k], (k + 1) * ext_x, 0), to_north)
            to_south = jnp.where(slot_of == k, roll(south[k], k * ext_x, 0), to_south)
        ys[rnd, 0, c, blk] = roll(to_north, 1, 1)
        ys[rnd, 1, c, blk] = roll(to_south, -1, 1)

    def beside_y(rnd, c, blk):
        at_south = jnp.where(first_lane, yr[rnd, 0, c, blk], ys[rnd, 0, c, blk])
        at_north = jnp.where(last_lane, yr[rnd, 1, c, blk], ys[rnd, 1, c, blk])
        return (
            [roll(at_south, -k * ext_x, 0) for k in range(per)],
            [roll(at_north, -(k + 1) * ext_x, 0) for k in range(per)],
        )

    first, last = 0, groups - 1
    comps = range(3)
    pen = 0.5 * PENALTY_SPEED

    def put_fluxes(s, blk):
        north, south = [[] for c in comps], [[] for c in comps]
        for n in range(per):
            i = blk * per + n
            for g in range(groups):
                h, p, m = (state[s, c, i, rows(g)] for c in comps)
                ih = 1.0 / h
                u, v = p * ih, m * ih
                inv_h[s, i, rows(g)] = ih
                vel_x[s, i, rows(g)] = u
                vel_y[s, i, rows(g)] = v
                pressure = 0.5 * h * h
                cross = p * v
                fx = (p, p * u + pressure, cross)
                fy = (m, cross, m * v + pressure)
                for c, q in enumerate((h, p, m)):
                    flux_x[c, i, rows(g)] = fx[c]
                    flux_y[c, i, rows(g)] = fy[c]
                    if g == last:
                        north[c].append(0.5 * fy[c] + pen * q)
                    if g == first:
                        south[c].append(pen * q - 0.5 * fy[c])
        for c in comps:
            pack_y(s, c, blk, north[c], south[c])

    def x_traces(s, c):
        east = [0.5 * flux_x[c, NP - 1, rows(g)] + pen * state[s, c, NP - 1, rows(g)] for g in range(groups)]
        west = [pen * state[s, c, 0, rows(g)] - 0.5 * flux_x[c, 0, rows(g)] for g in range(groups)]
        return east, west

    coefs = (0.5 * TIME_STEP, 0.5 * TIME_STEP, TIME_STEP)
    sums = (1.0, 2.0, 2.0, 1.0)
    final_weights = (TIME_STEP / 6.0, TIME_STEP / 3.0, TIME_STEP / 3.0, TIME_STEP / 6.0)

    def send_forward(s):
        for c in comps:
            pack_x(s, c, *x_traces(s, c))
        start(s, (EAST, WEST, NORTH, SOUTH))

    def set_up(i, _):
        for k in range(per):
            state[0, 1, i * per + k] = mom_ref[0, i * per + k]
            state[0, 2, i * per + k] = mom_ref[1, i * per + k]
        put_fluxes(0, i)
        return _

    for piece in arrive[3:]:
        piece.wait()
    lax.fori_loop(0, blocks, set_up, 0)
    pl.semaphore_wait(barrier, len(plane_peers) + len(line_peers))
    send_forward(0)

    for s in range(SECTIONS):
        def volume(blk, _):
            coef = load_coef(0)
            rough_g = rough_rows[...]
            for n in range(per):
                i = blk * per + n
                out = [minus_along_second(coef, [flux_y[c, i, rows(g)] for g in range(groups)]) for c in comps]
                for g in range(groups):
                    h, p, m = (state[s, c, i, rows(g)] for c in comps)
                    u, v = vel_x[s, i, rows(g)], vel_y[s, i, rows(g)]
                    speed = jnp.sqrt(u * u + v * v + SPEED_FLOOR)
                    kr = rough_g * speed * jnp.exp((-4.0 / 3.0) * jnp.log(h))
                    drag_r[s, i, rows(g)] = kr
                    k = rough_g * kr
                    tend[0, i, rows(g)] = out[0][g]
                    tend[1, i, rows(g)] = out[1][g] - k * p
                    tend[2, i, rows(g)] = out[2][g] - k * m
            return _

        lax.fori_loop(0, blocks, volume, 0)

        def volume_x(c, _):
            for g in range(groups):
                out = along_first(table, [flux_x[c, i, rows(g)] for i in range(NP)])
                for i in range(NP):
                    tend[c, i, rows(g)] -= out[i]
            return _

        lax.fori_loop(0, 3, volume_x, 0)

        await_all(s, (EAST, WEST, NORTH, SOUTH))
        for c in comps:
            east, west = x_traces(s, c)
            for g in range(groups):
                at_west, at_east = beside_x(s, c, g, east, west)
                q0, q7 = state[s, c, 0, rows(g)], state[s, c, NP - 1, rows(g)]
                f0, f7 = flux_x[c, 0, rows(g)], flux_x[c, NP - 1, rows(g)]
                tend[c, 0, rows(g)] += (inside[WEST]) * (at_west - (0.5 * f0 + pen * q0))
                tend[c, NP - 1, rows(g)] += (inside[EAST]) * (at_east - (pen * q7 - 0.5 * f7))

        def finish(blk, _):
            wet = wet_rows[s]
            for c in comps:
                at_south, at_north = beside_y(s, c, blk)
                for n in range(per):
                    i = blk * per + n
                    for g in range(groups):
                        slope = tend[c, i, rows(g)]
                        if g == first:
                            own = 0.5 * flux_y[c, i, rows(g)] + pen * state[s, c, i, rows(g)]
                            slope = slope + inside[SOUTH] * (at_south[n] - own)
                        if g == last:
                            own = pen * state[s, c, i, rows(g)] - 0.5 * flux_y[c, i, rows(g)]
                            slope = slope + inside[NORTH] * (at_north[n] - own)
                        slope = wet * slope
                        start_q = state[0, c, i, rows(g)]
                        if s == 0:
                            acc[c, i, rows(g)] = slope
                        elif s < SECTIONS - 1:
                            acc[c, i, rows(g)] += sums[s] * slope
                        if s < SECTIONS - 1:
                            state[s + 1, c, i, rows(g)] = start_q + coefs[s] * slope
                        elif c > 0:
                            total = acc[c, i, rows(g)] + slope
                            final = start_q + (TIME_STEP / 6.0) * total
                            seed = weight_ref[i, rows(g)] * final
                            final_adj[c - 1, i, rows(g)] = seed
                            adj_ref[c, i, rows(g)] = seed
                        else:
                            adj_ref[c, i, rows(g)] = jnp.zeros((SUB, ext_y), jnp.float32)
            if s < SECTIONS - 1:
                put_fluxes(s + 1, blk)
            else:
                put_cot(s, blk)
            return _

        def put_cot(s, blk):
            wet = wet_rows[s]
            for c in comps:
                north, south = [], []
                for n in range(per):
                    i = blk * per + n
                    for g in range(groups):
                        value = None
                        if c > 0:
                            value = final_weights[s] * final_adj[c - 1, i, rows(g)]
                        if s < SECTIONS - 1:
                            back = coefs[s] * later[c, i, rows(g)]
                            value = back if value is None else value + back
                        if value is None:
                            value = jnp.zeros((SUB, ext_y), jnp.float32)
                        value = wet * value
                        acc[c, i, rows(g)] = value
                        if g == last:
                            north.append(value)
                        if g == first:
                            south.append(value)
                pack_y(2 * SECTIONS - 1 - s, c, blk, north, south)

        lax.fori_loop(0, blocks, finish, 0)
        if s < SECTIONS - 1:
            send_forward(s + 1)

    def cot_faces(c):
        return (
            [acc[c, NP - 1, rows(g)] for g in range(groups)],
            [acc[c, 0, rows(g)] for g in range(groups)],
        )

    def plane_copy(k, peer):
        return pltpu.make_async_remote_copy(
            src_ref=zs.at[0], dst_ref=zr.at[k],
            send_sem=zsend_sem.at[k], recv_sem=zrecv_sem.at[k],
            device_id=peer, device_id_type=MESH,
        )

    def line_copy(k, peer):
        slot = plane + k
        return pltpu.make_async_remote_copy(
            src_ref=zs.at[1], dst_ref=zr.at[slot],
            send_sem=zsend_sem.at[slot], recv_sem=zrecv_sem.at[slot],
            device_id=peer, device_id_type=MESH,
        )

    for s in reversed(range(SECTIONS)):
        rnd = 2 * SECTIONS - 1 - s
        for c in comps:
            pack_x(rnd, c, *cot_faces(c))
        start(rnd, (EAST, WEST, NORTH, SOUTH))

        def drag_back(blk, _):
            rough_g = rough_rows[...]
            parts = []
            for n in range(per):
                i = blk * per + n
                for g in range(groups):
                    h, p, m = (state[s, c, i, rows(g)] for c in comps)
                    u, v, ih = vel_x[s, i, rows(g)], vel_y[s, i, rows(g)], inv_h[s, i, rows(g)]
                    kr = drag_r[s, i, rows(g)]
                    c1, c2 = acc[1, i, rows(g)], acc[2, i, rows(g)]
                    part = kr * (c1 * p + c2 * m)
                    parts.append(part)
                    k = rough_g * kr
                    e = rough_g * part * ih
                    square = u * u + v * v
                    eq = e / (square + SPEED_FLOOR)
                    tend[0, i, rows(g)] = (4.0 / 3.0) * e + eq * square
                    tend[1, i, rows(g)] = -(k * c1 + eq * u)
                    tend[2, i, rows(g)] = -(k * c2 + eq * v)
            zone_acc[...] += sum(parts)
            return _

        lax.fori_loop(0, blocks, drag_back, 0)

        if s == 0:
            total = zone_acc[...]
            shift = ext_x
            while shift < SUB:
                total = total + roll(total, shift, 0)
                shift *= 2
            total = -2.0 * total
            zones = lax.broadcasted_iota(jnp.int32, (ZONES, ext_y), 0)
            spot = jnp.zeros((ZONES, ext_y), jnp.float32)
            for e in range(ext_x):
                ids = jnp.broadcast_to(zone_ref[e:e + 1, :], (ZONES, ext_y))
                spot = spot + jnp.where(ids == zones, jnp.broadcast_to(total[e:e + 1], (ZONES, ext_y)), 0.0)
            per_zone = jnp.sum(spot, axis=1, keepdims=True)
            spots = lax.broadcasted_iota(jnp.int32, (ZONES, ext_y), 1)
            line = jnp.sum(jnp.where(zones == spots, jnp.broadcast_to(per_zone, (ZONES, ext_y)), 0.0), axis=0, keepdims=True)
            zs[0] = line
            for k, peer in plane_peers:
                plane_copy(k, peer).start()

        def volume_y(blk, _):
            coef = load_coef(1)
            for n in range(per):
                i = blk * per + n
                for c in comps:
                    out = minus_along_second(coef, [acc[c, i, rows(g)] for g in range(groups)])
                    for g in range(groups):
                        flux_y[c, i, rows(g)] = out[g]
            return _

        lax.fori_loop(0, blocks, volume_y, 0)

        def volume_back(c, _):
            for g in range(groups):
                out = along_first(-table.T, [acc[c, i, rows(g)] for i in range(NP)])
                for i in range(NP):
                    flux_x[c, i, rows(g)] = out[i]
            return _

        lax.fori_loop(0, 3, volume_back, 0)

        await_all(rnd, (EAST, WEST, NORTH, SOUTH))
        if s == 0:
            mine = zs[0]
            for k, peer in plane_peers:
                plane_copy(k, peer).wait_recv()
                mine = mine + zr[k]
            zs[1] = mine
            for k, peer in line_peers:
                line_copy(k, peer).start()
        for c in comps:
            east, west = cot_faces(c)
            for g in range(groups):
                at_west, at_east = beside_x(rnd, c, g, east, west)
                w_in, e_in = inside[WEST], inside[EAST]
                flux_x[c, 0, rows(g)] -= (0.5 * w_in) * (west[g] + at_west)
                tend[c, 0, rows(g)] += (pen * w_in) * (at_west - west[g])
                flux_x[c, NP - 1, rows(g)] += (0.5 * e_in) * (east[g] + at_east)
                tend[c, NP - 1, rows(g)] += (pen * e_in) * (at_east - east[g])

        def finish_back(blk, _):
            s_in, n_in = inside[SOUTH], inside[NORTH]
            beside = [beside_y(rnd, c, blk) for c in comps]
            for n in range(per):
                i = blk * per + n
                for g in range(groups):
                    a = [flux_x[c, i, rows(g)] for c in comps]
                    b = [flux_y[c, i, rows(g)] for c in comps]
                    out = [tend[c, i, rows(g)] for c in comps]
                    own = [acc[c, i, rows(g)] for c in comps]
                    for c in comps:
                        if g == first:
                            there = beside[c][0][n]
                            b[c] = b[c] - (0.5 * s_in) * (own[c] + there)
                            out[c] = out[c] + (pen * s_in) * (there - own[c])
                        if g == last:
                            there = beside[c][1][n]
                            b[c] = b[c] + (0.5 * n_in) * (own[c] + there)
                            out[c] = out[c] + (pen * n_in) * (there - own[c])
                    h = state[s, 0, i, rows(g)]
                    u, v = vel_x[s, i, rows(g)], vel_y[s, i, rows(g)]
                    cross = a[2] + b[1]
                    au, bv = a[1] * u, b[2] * v
                    cot = (
                        out[0] + (a[1] + b[2]) * h - au * u - bv * v - cross * (u * v),
                        out[1] + a[0] + 2.0 * au + cross * v,
                        out[2] + b[0] + 2.0 * bv + cross * u,
                    )
                    for c in comps:
                        adj_ref[c, i, rows(g)] += cot[c]
                        if s > 0:
                            later[c, i, rows(g)] = cot[c]
            if s > 0:
                put_cot(s - 1, blk)
            return _

        lax.fori_loop(0, blocks, finish_back, 0)

    whole = zs[1]
    for k, peer in line_peers:
        line_copy(k, peer).wait_recv()
        whole = whole + zr[plane + k]
    nodes = events * n_ev * ext_x * n_tx * ext_y * n_ty * NP * NP
    grad_ref[...] = whole[:, :ZONES] * (ZONES / (TIME_STEP * nodes))

    for rnd in range(2 * SECTIONS):
        for side in (EAST, WEST, NORTH, SOUTH):
            @pl.when(has[side])
            def _():
                copy(rnd, side).wait_send()
    for k, peer in plane_peers:
        plane_copy(k, peer).wait_send()
    for k, peer in line_peers:
        line_copy(k, peer).wait_send()


def local(axes, depth0, momentum0, obs_weight, wet_mask, zone_id, manning):
    ext_x, ext_y = depth0.shape[3:]
    rows = NP * ext_x
    field = (NP, rows, ext_y)
    rounds = 2 * SECTIONS
    slots = axes["ty"] * axes["ev"] + axes["tx"]
    f32 = jnp.float32
    vmem = pl.BlockSpec(memory_space=pltpu.VMEM)
    adjoint, grad = pl.pallas_call(
        functools.partial(kernel, axes, ext_x, depth0.shape[0]),
        out_shape=(
            jax.ShapeDtypeStruct((3,) + field, f32),
            jax.ShapeDtypeStruct((1, ZONES), f32),
        ),
        in_specs=[pl.BlockSpec(memory_space=pltpu.HBM)] * 6,
        out_specs=(vmem, vmem),
        scratch_shapes=[
            pltpu.VMEM((2,) + field, f32),
            pltpu.VMEM(field, f32),
            pltpu.VMEM(wet_mask.shape[1:], jnp.int32),
            pltpu.VMEM(zone_id.shape, jnp.int32),
            pltpu.SMEM(manning.shape, f32),
            pltpu.SemaphoreType.DMA((6,)),
            pltpu.VMEM((SECTIONS, 3) + field, f32),
            pltpu.VMEM((SECTIONS,) + field, f32),
            pltpu.VMEM((SECTIONS,) + field, f32),
            pltpu.VMEM((SECTIONS,) + field, f32),
            pltpu.VMEM((SECTIONS,) + field, f32),
            pltpu.VMEM((3,) + field, f32),
            pltpu.VMEM((3,) + field, f32),
            pltpu.VMEM((3,) + field, f32),
            pltpu.VMEM((3,) + field, f32),
            pltpu.VMEM((2,) + field, f32),
            pltpu.VMEM((3,) + field, f32),
            pltpu.VMEM((SECTIONS, SUB, ext_y), f32),
            pltpu.VMEM((SUB, ext_y), f32),
            pltpu.VMEM((2, ext_x, ext_x, SUB // ext_x, SUB, ext_y), f32),
            pltpu.VMEM((SUB, ext_y), f32),
            pltpu.VMEM((rounds, 2, 3, SUB, ext_y), f32),
            pltpu.VMEM((rounds, 2, 3, SUB, ext_y), f32),
            pltpu.VMEM((rounds, 2, 3, NP // (SUB // ext_x), SUB, ext_y), f32),
            pltpu.VMEM((rounds, 2, 3, NP // (SUB // ext_x), SUB, ext_y), f32),
            pltpu.VMEM((2, 1, ext_y), f32),
            pltpu.VMEM((slots, 1, ext_y), f32),
            pltpu.SemaphoreType.DMA((rounds, 4)),
            pltpu.SemaphoreType.DMA((rounds, 4)),
            pltpu.SemaphoreType.DMA((slots,)),
            pltpu.SemaphoreType.DMA((slots,)),
        ],
        compiler_params=pltpu.CompilerParams(
            collective_id=0, has_side_effects=True, vmem_limit_bytes=32 * 1024 * 1024
        ),
    )(
        depth0.reshape(field),
        momentum0.reshape((2,) + field),
        obs_weight.reshape(field),
        wet_mask.reshape(wet_mask.shape[1:]),
        zone_id,
        manning,
    )
    return adjoint.reshape((1, 3, NP, NP, ext_x, ext_y)), grad.reshape((ZONES,))


def solution(mesh):
    in_specs = (
        P(("basin", "ev"), None, None, "tx", "ty"),
        P(("basin", "ev"), None, None, None, "tx", "ty"),
        P(("basin", "ev"), None, None, "tx", "ty"),
        P(("basin", "ev"), None, "tx", "ty"),
        P(("basin", "tx"), "ty"),
        P("basin"),
    )
    out_specs = (P(("basin", "ev"), None, None, None, "tx", "ty"), P("basin"))
    return jax.shard_map(
        functools.partial(local, dict(mesh.shape)),
        mesh=mesh, in_specs=in_specs, out_specs=out_specs, check_vma=False,
    )
```

```python
import functools

import jax
import jax.numpy as jnp
import numpy as np
from jax import lax
from jax.experimental import pallas as pl
from jax.experimental.pallas import tpu as pltpu
from jax.sharding import PartitionSpec as P

NP = 8
SECTIONS = 4
ZONES = 32
SUB = 8

PENALTY_SPEED = 4.0
TIME_STEP = 0.0005
SPEED_FLOOR = 0.01
MESH = pl.DeviceIdType.MESH
EAST, WEST, NORTH, SOUTH = range(4)
DIRECT = 32


def node_tables():
    points = -np.cos(np.pi * np.arange(NP) / (NP - 1))
    identity = np.eye(NP)
    differ = points[:, None] - points[None, :] + identity
    barycentric = 1.0 / np.prod(differ, axis=1)
    derivative = barycentric[None, :] / barycentric[:, None] / differ * (1.0 - identity)
    derivative = derivative - identity * derivative.sum(axis=1)[:, None]
    order = NP - 1
    end_weight = 1.0 / (order * order)
    return (derivative, float(1.0 / end_weight))


def along_first(table, slabs):
    half = NP // 2
    even = [slabs[k] + slabs[NP - 1 - k] for k in range(half)]
    odd = [slabs[k] - slabs[NP - 1 - k] for k in range(half)]
    out = [None] * NP
    for a in range(half):
        on_even = sum(float(0.5 * (table[a, k] + table[a, NP - 1 - k])) * even[k] for k in range(half))
        on_odd = sum(float(0.5 * (table[a, k] - table[a, NP - 1 - k])) * odd[k] for k in range(half))
        out[a] = on_odd + on_even
        out[NP - 1 - a] = on_odd - on_even
    return out


def kernel(
    axes, ext_x, events,
    depth_hbm, mom_hbm, weight_hbm, wet_hbm, zone_hbm, manning_hbm,
    adj_hbm, grad_ref,
    adj_ref, out_sem, mom_ref, weight_ref, wet_ref, zone_ref, manning_ref, in_sem,
    state, vel_x, vel_y, inv_h, drag_r, flux_x, flux_y, tend, acc, final_adj, later,
    wet_rows, rough_rows, coef_y, zone_acc,
    xs, xr, ys, yr, zs, zr, send_sem, recv_sem, zsend_sem, zrecv_sem,
):
    table, lift = node_tables()
    n_tx, n_ty, n_ev = axes["tx"], axes["ty"], axes["ev"]
    tx, ty, ev = lax.axis_index("tx"), lax.axis_index("ty"), lax.axis_index("ev")
    ext_y = depth_hbm.shape[-1]
    groups = ext_x
    step = ext_x
    per = SUB // ext_x
    blocks = NP // per
    order = [0, NP - 1] + list(range(1, NP - 1))
    order = order if per >= 2 else list(range(NP))
    edge_i = (0, NP - 1)
    has = {EAST: tx < n_tx - 1, WEST: tx > 0, NORTH: ty < n_ty - 1, SOUTH: ty > 0}
    target = {EAST: {"tx": tx + 1}, WEST: {"tx": tx - 1}, NORTH: {"ty": ty + 1}, SOUTH: {"ty": ty - 1}}
    opposite = {EAST: WEST, WEST: EAST, NORTH: SOUTH, SOUTH: NORTH}

    arrive = [
        pltpu.make_async_copy(source, target_ref, in_sem.at[n])
        for n, (source, target_ref) in enumerate((
            (zone_hbm, zone_ref), (manning_hbm, manning_ref), (wet_hbm, wet_ref),
            (depth_hbm, state.at[0, 0]), (mom_hbm, mom_ref), (weight_hbm, weight_ref),
        ))
    ]
    for piece in arrive:
        piece.start()

    barrier = pltpu.get_barrier_semaphore()
    sizes = {"ty": n_ty, "ev": n_ev, "tx": n_tx}
    all_names = ("ty", "ev", "tx")
    direct = n_ty * n_ev * n_tx <= DIRECT
    phases = []
    slots = 0
    for names in ((all_names,) if direct else (all_names[:2], all_names[2:])):
        count = int(np.prod([sizes[name] for name in names]))
        here = 0
        for name in names:
            here = here * sizes[name] + lax.axis_index(name)
        peers = []
        for k in range(1, count):
            rest = lax.rem(here + k, count)
            peer = {}
            for name in reversed(names):
                peer[name] = lax.rem(rest, sizes[name])
                rest = rest // sizes[name]
            peers.append((slots, peer))
            slots += 1
        phases.append(peers)
    for peers in phases:
        for _, peer in peers:
            pl.semaphore_signal(barrier, inc=1, device_id=peer, device_id_type=MESH)

    sub = lax.broadcasted_iota(jnp.int32, (SUB, ext_y), 0)
    lane = lax.broadcasted_iota(jnp.int32, (SUB, ext_y), 1)
    elem = lax.rem(sub, ext_x)

    def flag(yes):
        return jnp.where(yes, 1, 0)

    zero = jnp.float32(0.0)
    inside = {
        WEST: jnp.where((elem == 0) & (flag(has[WEST]) == 0), zero, lift),
        EAST: jnp.where((elem == ext_x - 1) & (flag(has[EAST]) == 0), zero, lift),
        SOUTH: jnp.where((sub >= ext_x) | ((lane == 0) & (flag(has[SOUTH]) == 0)), zero, lift),
        NORTH: jnp.where((sub < SUB - ext_x) | ((lane == ext_y - 1) & (flag(has[NORTH]) == 0)), zero, lift),
    }
    first_elem = (elem == 0) & (flag(has[WEST]) == 1)
    last_elem = (elem == ext_x - 1) & (flag(has[EAST]) == 1)
    first_lane = (lane == 0) & (flag(has[SOUTH]) == 1)
    last_lane = (lane == ext_y - 1) & (flag(has[NORTH]) == 1)

    def spread(rows):
        out = jnp.broadcast_to(rows[0:1], (SUB, ext_y))
        for e in range(1, ext_x):
            out = jnp.where(elem == e, jnp.broadcast_to(rows[e:e + 1], (SUB, ext_y)), out)
        return out

    for t, mat in enumerate((table, table.T)):
        for g in range(groups):
            for h in range(groups):
                for k in range(SUB // step):
                    column = jnp.zeros((SUB, ext_y), jnp.float32)
                    for r in range(SUB):
                        a = (SUB * g + r) // ext_x
                        b = (SUB * h + (r - k * step) % SUB) // ext_x
                        column = jnp.where(sub == r, jnp.float32(-mat[a, b]), column)
                    coef_y[t, g, h, k] = column
    for piece in arrive[:3]:
        piece.wait()
    for s in range(SECTIONS):
        wet_rows[s] = spread(wet_ref[s].astype(jnp.float32))
    zone = spread(zone_ref[...])
    rough = jnp.zeros((SUB, ext_y), jnp.float32)
    for z in range(ZONES):
        rough = jnp.where(zone == z, manning_ref[z], rough)
    rough_rows[...] = rough

    zone_acc[...] = jnp.zeros((SUB, ext_y), jnp.float32)

    def rows(g):
        return pl.ds(SUB * g, SUB)

    def roll(value, shift, axis):
        size = value.shape[axis]
        shift = shift % size
        return value if shift == 0 else pltpu.roll(value, shift, axis)

    def load_coef(t):
        return [[[coef_y[t, g, h, k] for k in range(per)] for h in range(groups)] for g in range(groups)]

    def minus_along_second(coef, source):
        turned = [[roll(source[h], k * step, 0) for k in range(per)] for h in range(groups)]
        return [
            sum(coef[g][h][k] * turned[h][k] for h in range(groups) for k in range(per))
            for g in range(groups)
        ]

    def copy(rnd, side, blk=None):
        if side in (EAST, WEST):
            source, there, sem = xs.at[rnd, side], xr.at[rnd, side], side
        else:
            source, there = ys.at[rnd, side - 2, blk], yr.at[rnd, side - 2, blk]
            sem = 2 + (side - 2) * blocks + blk
        return pltpu.make_async_remote_copy(
            src_ref=source,
            dst_ref=there,
            send_sem=send_sem.at[rnd, sem],
            recv_sem=recv_sem.at[rnd, sem],
            device_id=target[side],
            device_id_type=MESH,
        )

    def start(rnd, sides, blk=None):
        for side in sides:
            @pl.when(has[side])
            def _():
                copy(rnd, side, blk).start()

    def await_from(rnd, sides, blk=None):
        for side in sides:
            @pl.when(has[opposite[side]])
            def _():
                copy(rnd, side, blk).wait_recv()

    def pack_x(rnd, c, east, west):
        to_east, to_west = east[0], west[0]
        for g in range(1, groups):
            to_east = jnp.where(elem == ext_x - 1 - g, roll(east[g], -g, 0), to_east)
            to_west = jnp.where(elem == g, roll(west[g], g, 0), to_west)
        xs[rnd, EAST, c] = to_east
        xs[rnd, WEST, c] = to_west

    def beside_x(rnd, c, g, east, west):
        from_west, from_east = xr[rnd, EAST, c], xr[rnd, WEST, c]
        at_west = jnp.where(first_elem, roll(from_west, -(ext_x - 1 - g), 0), roll(east[g], 1, 0))
        at_east = jnp.where(last_elem, roll(from_east, ext_x - 1 - g, 0), roll(west[g], -1, 0))
        return at_west, at_east

    slot_of = sub // ext_x

    def pack_y(rnd, c, blk, north, south):
        to_north, to_south = roll(north[0], ext_x, 0), south[0]
        for k in range(1, per):
            to_north = jnp.where(slot_of == k, roll(north[k], (k + 1) * ext_x, 0), to_north)
            to_south = jnp.where(slot_of == k, roll(south[k], k * ext_x, 0), to_south)
        ys[rnd, 0, blk, c] = roll(to_north, 1, 1)
        ys[rnd, 1, blk, c] = roll(to_south, -1, 1)

    def beside_y(rnd, c, i):
        blk, k = divmod(order.index(i), per)
        at_south = jnp.where(first_lane, yr[rnd, 0, blk, c], ys[rnd, 0, blk, c])
        at_north = jnp.where(last_lane, yr[rnd, 1, blk, c], ys[rnd, 1, blk, c])
        return roll(at_south, -k * ext_x, 0), roll(at_north, -(k + 1) * ext_x, 0)

    first, last = 0, groups - 1
    comps = range(3)
    pen = 0.5 * PENALTY_SPEED

    def put_fluxes(s, i):
        for g in range(groups):
            h, p, m = (state[s, c, i, rows(g)] for c in comps)
            ih = 1.0 / h
            u, v = p * ih, m * ih
            inv_h[s, i, rows(g)] = ih
            vel_x[s, i, rows(g)] = u
            vel_y[s, i, rows(g)] = v
            pressure = 0.5 * h * h
            cross = p * v
            fx = (p, p * u + pressure, cross)
            fy = (m, cross, m * v + pressure)
            for c in comps:
                flux_x[c, i, rows(g)] = fx[c]
                flux_y[c, i, rows(g)] = fy[c]
            if g == last:
                north = [0.5 * fy[c] + pen * q for c, q in enumerate((h, p, m))]
            if g == first:
                south = [pen * q - 0.5 * fy[c] for c, q in enumerate((h, p, m))]
        return north, south

    def run_columns(rnd, arrived, one_column, x_pack):
        faces = {}
        sweep = list(range(blocks))
        if arrived is not None:
            sweep = sweep[::-1]
        edge_sweep = [blk for blk in sweep if blk in edge_blocks]
        for blk in sweep:
            members = order[blk * per:(blk + 1) * per]
            inner = [i for i in members if i not in edge_i]
            edge = [i for i in members if i in edge_i]
            if arrived is not None:
                await_from(arrived, (NORTH, SOUTH), blk)
                for i in inner:
                    faces[i] = one_column(i)
                if blk == edge_sweep[0]:
                    await_from(arrived, (EAST, WEST))
            for i in edge:
                faces[i] = one_column(i)
            if rnd is not None and blk == edge_sweep[-1]:
                x_pack()
                start(rnd, (EAST, WEST))
            if arrived is None:
                for i in inner:
                    faces[i] = one_column(i)
            if rnd is not None:
                for c in comps:
                    pack_y(rnd, c, blk, [faces[i][0][c] for i in members], [faces[i][1][c] for i in members])
                start(rnd, (NORTH, SOUTH), blk)

    edge_blocks = sorted({order.index(i) // per for i in edge_i})

    def x_traces(s, c):
        east = [0.5 * flux_x[c, NP - 1, rows(g)] + pen * state[s, c, NP - 1, rows(g)] for g in range(groups)]
        west = [pen * state[s, c, 0, rows(g)] - 0.5 * flux_x[c, 0, rows(g)] for g in range(groups)]
        return east, west

    coefs = (0.5 * TIME_STEP, 0.5 * TIME_STEP, TIME_STEP)
    sums = (1.0, 2.0, 2.0, 1.0)
    final_weights = (TIME_STEP / 6.0, TIME_STEP / 3.0, TIME_STEP / 3.0, TIME_STEP / 6.0)

    def pack_forward(s):
        for c in comps:
            pack_x(s, c, *x_traces(s, c))

    def pack_back(rnd):
        for c in comps:
            pack_x(rnd, c, *cot_faces(c))

    def cot_faces(c):
        return (
            [acc[c, NP - 1, rows(g)] for g in range(groups)],
            [acc[c, 0, rows(g)] for g in range(groups)],
        )

    def set_up(i):
        state[0, 1, i] = mom_ref[0, i]
        state[0, 2, i] = mom_ref[1, i]
        return put_fluxes(0, i)

    for piece in arrive[3:]:
        piece.wait()
    pl.semaphore_wait(barrier, slots)
    run_columns(0, None, set_up, lambda: pack_forward(0))

    for s in range(SECTIONS):
        def volume(blk, _):
            coef = load_coef(0)
            rough_g = rough_rows[...]
            for n in range(per):
                i = blk * per + n
                out = [minus_along_second(coef, [flux_y[c, i, rows(g)] for g in range(groups)]) for c in comps]
                for g in range(groups):
                    h, p, m = (state[s, c, i, rows(g)] for c in comps)
                    u, v = vel_x[s, i, rows(g)], vel_y[s, i, rows(g)]
                    speed = jnp.sqrt(u * u + v * v + SPEED_FLOOR)
                    kr = rough_g * speed * jnp.exp((-4.0 / 3.0) * jnp.log(h))
                    drag_r[s, i, rows(g)] = kr
                    k = rough_g * kr
                    tend[0, i, rows(g)] = out[0][g]
                    tend[1, i, rows(g)] = out[1][g] - k * p
                    tend[2, i, rows(g)] = out[2][g] - k * m
            return _

        lax.fori_loop(0, blocks, volume, 0)

        def volume_x(c, _):
            for g in range(groups):
                out = along_first(table, [flux_x[c, i, rows(g)] for i in range(NP)])
                for i in range(NP):
                    tend[c, i, rows(g)] -= out[i]
            return _

        lax.fori_loop(0, 3, volume_x, 0)

        def finish(i):
            wet = wet_rows[s]
            for c in comps:
                at_south, at_north = beside_y(s, c, i)
                for g in range(groups):
                    slope = tend[c, i, rows(g)]
                    q = state[s, c, i, rows(g)]
                    if i in edge_i:
                        at_west, at_east = beside_x(s, c, g, *old_x[c])
                        if i == 0:
                            slope = slope + inside[WEST] * (at_west - (0.5 * flux_x[c, i, rows(g)] + pen * q))
                        else:
                            slope = slope + inside[EAST] * (at_east - (pen * q - 0.5 * flux_x[c, i, rows(g)]))
                    if g == first:
                        slope = slope + inside[SOUTH] * (at_south - (0.5 * flux_y[c, i, rows(g)] + pen * q))
                    if g == last:
                        slope = slope + inside[NORTH] * (at_north - (pen * q - 0.5 * flux_y[c, i, rows(g)]))
                    slope = wet * slope
                    start_q = state[0, c, i, rows(g)]
                    if s == 0:
                        acc[c, i, rows(g)] = slope
                    elif s < SECTIONS - 1:
                        acc[c, i, rows(g)] += sums[s] * slope
                    if s < SECTIONS - 1:
                        state[s + 1, c, i, rows(g)] = start_q + coefs[s] * slope
                    elif c > 0:
                        total = acc[c, i, rows(g)] + slope
                        final = start_q + (TIME_STEP / 6.0) * total
                        seed = weight_ref[i, rows(g)] * final
                        final_adj[c - 1, i, rows(g)] = seed
                        adj_ref[c, i, rows(g)] = seed
                    else:
                        adj_ref[c, i, rows(g)] = jnp.zeros((SUB, ext_y), jnp.float32)
            if s < SECTIONS - 1:
                return put_fluxes(s + 1, i)
            return put_cot(s, i)

        def put_cot(s, i):
            wet = wet_rows[s]
            north, south = [], []
            for c in comps:
                for g in range(groups):
                    value = None
                    if c > 0:
                        value = final_weights[s] * final_adj[c - 1, i, rows(g)]
                    if s < SECTIONS - 1:
                        back = coefs[s] * later[c, i, rows(g)]
                        value = back if value is None else value + back
                    if value is None:
                        value = jnp.zeros((SUB, ext_y), jnp.float32)
                    value = wet * value
                    acc[c, i, rows(g)] = value
                    if g == last:
                        north.append(value)
                    if g == first:
                        south.append(value)
            return north, south

        old_x = [x_traces(s, c) for c in comps]
        if s < SECTIONS - 1:
            run_columns(s + 1, s, finish, lambda: pack_forward(s + 1))
        else:
            run_columns(SECTIONS, s, finish, lambda: pack_back(SECTIONS))

    def zone_copy(n, slot, peer):
        return pltpu.make_async_remote_copy(
            src_ref=zs.at[n], dst_ref=zr.at[slot],
            send_sem=zsend_sem.at[slot], recv_sem=zrecv_sem.at[slot],
            device_id=peer, device_id_type=MESH,
        )

    def zone_start(n):
        for slot, peer in phases[n]:
            zone_copy(n, slot, peer).start()

    def zone_end(n):
        total = zs[n]
        for slot, peer in phases[n]:
            zone_copy(n, slot, peer).wait_recv()
            total = total + zr[slot]
        return total

    def write_out(n, c, first_i, count):
        part = pl.ds(first_i, count)
        return pltpu.make_async_copy(adj_ref.at[c, part], adj_hbm.at[c, part], out_sem.at[n, c])

    for s in reversed(range(SECTIONS)):
        rnd = 2 * SECTIONS - 1 - s
        def drag_back(blk, _):
            rough_g = rough_rows[...]
            parts = []
            for n in range(per):
                i = blk * per + n
                for g in range(groups):
                    h, p, m = (state[s, c, i, rows(g)] for c in comps)
                    u, v, ih = vel_x[s, i, rows(g)], vel_y[s, i, rows(g)], inv_h[s, i, rows(g)]
                    kr = drag_r[s, i, rows(g)]
                    c1, c2 = acc[1, i, rows(g)], acc[2, i, rows(g)]
                    part = kr * (c1 * p + c2 * m)
                    parts.append(part)
                    k = rough_g * kr
                    e = rough_g * part * ih
                    square = u * u + v * v
                    eq = e / (square + SPEED_FLOOR)
                    tend[0, i, rows(g)] = (4.0 / 3.0) * e + eq * square
                    tend[1, i, rows(g)] = -(k * c1 + eq * u)
                    tend[2, i, rows(g)] = -(k * c2 + eq * v)
            zone_acc[...] += sum(parts)
            return _

        lax.fori_loop(0, blocks, drag_back, 0)

        if s == 0:
            total = zone_acc[...]
            shift = ext_x
            while shift < SUB:
                total = total + roll(total, shift, 0)
                shift *= 2
            total = -2.0 * total
            zones = lax.broadcasted_iota(jnp.int32, (ZONES, ext_y), 0)
            spot = jnp.zeros((ZONES, ext_y), jnp.float32)
            for e in range(ext_x):
                ids = jnp.broadcast_to(zone_ref[e:e + 1, :], (ZONES, ext_y))
                spot = spot + jnp.where(ids == zones, jnp.broadcast_to(total[e:e + 1], (ZONES, ext_y)), 0.0)
            per_zone = jnp.sum(spot, axis=1, keepdims=True)
            spots = lax.broadcasted_iota(jnp.int32, (ZONES, ext_y), 1)
            line = jnp.sum(jnp.where(zones == spots, jnp.broadcast_to(per_zone, (ZONES, ext_y)), 0.0), axis=0, keepdims=True)
            zs[0] = line
            zone_start(0)

        def volume_y(blk, _):
            coef = load_coef(1)
            for n in range(per):
                i = blk * per + n
                for c in comps:
                    out = minus_along_second(coef, [acc[c, i, rows(g)] for g in range(groups)])
                    for g in range(groups):
                        flux_y[c, i, rows(g)] = out[g]
            return _

        lax.fori_loop(0, blocks, volume_y, 0)

        def volume_back(c, _):
            for g in range(groups):
                out = along_first(-table.T, [acc[c, i, rows(g)] for i in range(NP)])
                for i in range(NP):
                    flux_x[c, i, rows(g)] = out[i]
            return _

        lax.fori_loop(0, 3, volume_back, 0)

        old_x = [cot_faces(c) for c in comps]

        def finish_back(i):
            s_in, n_in, w_in, e_in = inside[SOUTH], inside[NORTH], inside[WEST], inside[EAST]
            beside = [beside_y(rnd, c, i) for c in comps]
            for g in range(groups):
                a = [flux_x[c, i, rows(g)] for c in comps]
                b = [flux_y[c, i, rows(g)] for c in comps]
                out = [tend[c, i, rows(g)] for c in comps]
                own = [acc[c, i, rows(g)] for c in comps]
                for c in comps:
                    if i in edge_i:
                        at_west, at_east = beside_x(rnd, c, g, *old_x[c])
                        if i == 0:
                            a[c] = a[c] - (0.5 * w_in) * (own[c] + at_west)
                            out[c] = out[c] + (pen * w_in) * (at_west - own[c])
                        else:
                            a[c] = a[c] + (0.5 * e_in) * (own[c] + at_east)
                            out[c] = out[c] + (pen * e_in) * (at_east - own[c])
                    if g == first:
                        there = beside[c][0]
                        b[c] = b[c] - (0.5 * s_in) * (own[c] + there)
                        out[c] = out[c] + (pen * s_in) * (there - own[c])
                    if g == last:
                        there = beside[c][1]
                        b[c] = b[c] + (0.5 * n_in) * (own[c] + there)
                        out[c] = out[c] + (pen * n_in) * (there - own[c])
                h = state[s, 0, i, rows(g)]
                u, v = vel_x[s, i, rows(g)], vel_y[s, i, rows(g)]
                cross = a[2] + b[1]
                au, bv = a[1] * u, b[2] * v
                cot = (
                    out[0] + (a[1] + b[2]) * h - au * u - bv * v - cross * (u * v),
                    out[1] + a[0] + 2.0 * au + cross * v,
                    out[2] + b[0] + 2.0 * bv + cross * u,
                )
                for c in comps:
                    adj_ref[c, i, rows(g)] += cot[c]
                    if s > 0:
                        later[c, i, rows(g)] = cot[c]
            if s > 0:
                return put_cot(s - 1, i)

        if s > 0:
            run_columns(rnd + 1, rnd, finish_back, lambda: pack_back(rnd + 1))
        else:
            run_columns(None, rnd, finish_back, None)

    writes = [write_out(0, c, 0, NP) for c in comps]
    for write in writes:
        write.start()
    whole = zone_end(0)
    if not direct:
        zs[1] = whole
        zone_start(1)
        whole = zone_end(1)
    nodes = events * n_ev * ext_x * n_tx * ext_y * n_ty * NP * NP
    grad_ref[...] = whole[:, :ZONES] * (ZONES / (TIME_STEP * nodes))

    for rnd in range(2 * SECTIONS):
        for side in (EAST, WEST):
            @pl.when(has[side])
            def _():
                copy(rnd, side).wait_send()
        for side in (NORTH, SOUTH):
            @pl.when(has[side])
            def _():
                for blk in range(blocks):
                    copy(rnd, side, blk).wait_send()
    for n, peers in enumerate(phases):
        for slot, peer in peers:
            zone_copy(n, slot, peer).wait_send()
    for write in writes:
        write.wait()


def local(axes, depth0, momentum0, obs_weight, wet_mask, zone_id, manning):
    ext_x, ext_y = depth0.shape[3:]
    rows = NP * ext_x
    field = (NP, rows, ext_y)
    rounds = 2 * SECTIONS
    slots = axes["ty"] * axes["ev"] * axes["tx"]
    if slots > DIRECT:
        slots = axes["ty"] * axes["ev"] + axes["tx"]
    f32 = jnp.float32
    vmem = pl.BlockSpec(memory_space=pltpu.VMEM)
    adjoint, grad = pl.pallas_call(
        functools.partial(kernel, axes, ext_x, depth0.shape[0]),
        out_shape=(
            jax.ShapeDtypeStruct((3,) + field, f32),
            jax.ShapeDtypeStruct((1, ZONES), f32),
        ),
        in_specs=[pl.BlockSpec(memory_space=pltpu.HBM)] * 6,
        out_specs=(pl.BlockSpec(memory_space=pltpu.HBM), vmem),
        scratch_shapes=[
            pltpu.VMEM((3,) + field, f32),
            pltpu.SemaphoreType.DMA((1, 3)),
            pltpu.VMEM((2,) + field, f32),
            pltpu.VMEM(field, f32),
            pltpu.VMEM(wet_mask.shape[1:], jnp.int32),
            pltpu.VMEM(zone_id.shape, jnp.int32),
            pltpu.SMEM(manning.shape, f32),
            pltpu.SemaphoreType.DMA((6,)),
            pltpu.VMEM((SECTIONS, 3) + field, f32),
            pltpu.VMEM((SECTIONS,) + field, f32),
            pltpu.VMEM((SECTIONS,) + field, f32),
            pltpu.VMEM((SECTIONS,) + field, f32),
            pltpu.VMEM((SECTIONS,) + field, f32),
            pltpu.VMEM((3,) + field, f32),
            pltpu.VMEM((3,) + field, f32),
            pltpu.VMEM((3,) + field, f32),
            pltpu.VMEM((3,) + field, f32),
            pltpu.VMEM((2,) + field, f32),
            pltpu.VMEM((3,) + field, f32),
            pltpu.VMEM((SECTIONS, SUB, ext_y), f32),
            pltpu.VMEM((SUB, ext_y), f32),
            pltpu.VMEM((2, ext_x, ext_x, SUB // ext_x, SUB, ext_y), f32),
            pltpu.VMEM((SUB, ext_y), f32),
            pltpu.VMEM((rounds, 2, 3, SUB, ext_y), f32),
            pltpu.VMEM((rounds, 2, 3, SUB, ext_y), f32),
            pltpu.VMEM((rounds, 2, NP // (SUB // ext_x), 3, SUB, ext_y), f32),
            pltpu.VMEM((rounds, 2, NP // (SUB // ext_x), 3, SUB, ext_y), f32),
            pltpu.VMEM((2, 1, ext_y), f32),
            pltpu.VMEM((slots, 1, ext_y), f32),
            pltpu.SemaphoreType.DMA((rounds, 2 + 2 * (NP // (SUB // ext_x)))),
            pltpu.SemaphoreType.DMA((rounds, 2 + 2 * (NP // (SUB // ext_x)))),
            pltpu.SemaphoreType.DMA((slots,)),
            pltpu.SemaphoreType.DMA((slots,)),
        ],
        compiler_params=pltpu.CompilerParams(
            collective_id=0, has_side_effects=True, vmem_limit_bytes=60 * 1024 * 1024
        ),
    )(
        depth0.reshape(field),
        momentum0.reshape((2,) + field),
        obs_weight.reshape(field),
        wet_mask.reshape(wet_mask.shape[1:]),
        zone_id,
        manning,
    )
    return adjoint.reshape((1, 3, NP, NP, ext_x, ext_y)), grad.reshape((ZONES,))


def solution(mesh):
    in_specs = (
        P(("basin", "ev"), None, None, "tx", "ty"),
        P(("basin", "ev"), None, None, None, "tx", "ty"),
        P(("basin", "ev"), None, None, "tx", "ty"),
        P(("basin", "ev"), None, "tx", "ty"),
        P(("basin", "tx"), "ty"),
        P("basin"),
    )
    out_specs = (P(("basin", "ev"), None, None, None, "tx", "ty"), P("basin"))
    return jax.shard_map(
        functools.partial(local, dict(mesh.shape)),
        mesh=mesh, in_specs=in_specs, out_specs=out_specs, check_vma=False,
    )
```

```python
import functools

import jax
import jax.numpy as jnp
import numpy as np
from jax import lax
from jax.experimental import pallas as pl
from jax.experimental.pallas import tpu as pltpu
from jax.sharding import PartitionSpec as P

NP = 8
SECTIONS = 4
ZONES = 32
SUB = 8

PENALTY_SPEED = 4.0
TIME_STEP = 0.0005
SPEED_FLOOR = 0.01
MESH = pl.DeviceIdType.MESH
EAST, WEST, NORTH, SOUTH = range(4)
DIRECT = 32


def node_tables():
    points = -np.cos(np.pi * np.arange(NP) / (NP - 1))
    identity = np.eye(NP)
    differ = points[:, None] - points[None, :] + identity
    barycentric = 1.0 / np.prod(differ, axis=1)
    derivative = barycentric[None, :] / barycentric[:, None] / differ * (1.0 - identity)
    derivative = derivative - identity * derivative.sum(axis=1)[:, None]
    order = NP - 1
    end_weight = 1.0 / (order * order)
    return (derivative, float(1.0 / end_weight))


def along_first(table, slabs):
    half = NP // 2
    even = [slabs[k] + slabs[NP - 1 - k] for k in range(half)]
    odd = [slabs[k] - slabs[NP - 1 - k] for k in range(half)]
    out = [None] * NP
    for a in range(half):
        on_even = sum(float(0.5 * (table[a, k] + table[a, NP - 1 - k])) * even[k] for k in range(half))
        on_odd = sum(float(0.5 * (table[a, k] - table[a, NP - 1 - k])) * odd[k] for k in range(half))
        out[a] = on_odd + on_even
        out[NP - 1 - a] = on_odd - on_even
    return out


def kernel(
    axes, ext_x, events,
    depth_hbm, mom_hbm, weight_hbm, wet_hbm, zone_hbm, manning_hbm,
    adj_hbm, grad_ref,
    adj_ref, out_sem, mom_ref, weight_ref, wet_ref, zone_ref, manning_ref, in_sem,
    state, vel_x, vel_y, inv_h, drag_r, flux_x, flux_y, tend, acc, final_adj, later,
    wet_rows, rough_rows, coef_y, zone_acc,
    xs, xr, ys, yr, zs, zr, send_sem, recv_sem, zsend_sem, zrecv_sem,
):
    table, lift = node_tables()
    n_tx, n_ty, n_ev = axes["tx"], axes["ty"], axes["ev"]
    tx, ty, ev = lax.axis_index("tx"), lax.axis_index("ty"), lax.axis_index("ev")
    ext_y = depth_hbm.shape[-1]
    groups = ext_x
    step = ext_x
    per = SUB // ext_x
    blocks = NP // per
    order = [0, NP - 1] + list(range(1, NP - 1))
    order = order if per >= 2 else list(range(NP))
    edge_i = (0, NP - 1)
    has = {EAST: tx < n_tx - 1, WEST: tx > 0, NORTH: ty < n_ty - 1, SOUTH: ty > 0}
    target = {EAST: {"tx": tx + 1}, WEST: {"tx": tx - 1}, NORTH: {"ty": ty + 1}, SOUTH: {"ty": ty - 1}}
    opposite = {EAST: WEST, WEST: EAST, NORTH: SOUTH, SOUTH: NORTH}

    arrive = [
        pltpu.make_async_copy(source, target_ref, in_sem.at[n])
        for n, (source, target_ref) in enumerate((
            (zone_hbm, zone_ref), (manning_hbm, manning_ref), (wet_hbm, wet_ref),
            (depth_hbm, state.at[0, 0]), (mom_hbm, mom_ref), (weight_hbm, weight_ref),
        ))
    ]
    for piece in arrive:
        piece.start()

    barrier = pltpu.get_barrier_semaphore()
    sizes = {"ty": n_ty, "ev": n_ev, "tx": n_tx}
    all_names = ("ty", "ev", "tx")
    direct = n_ty * n_ev * n_tx <= DIRECT
    phases = []
    slots = 0
    for names in ((all_names,) if direct else (all_names[:2], all_names[2:])):
        count = int(np.prod([sizes[name] for name in names]))
        here = 0
        for name in names:
            here = here * sizes[name] + lax.axis_index(name)
        peers = []
        for k in range(1, count):
            rest = lax.rem(here + k, count)
            peer = {}
            for name in reversed(names):
                peer[name] = lax.rem(rest, sizes[name])
                rest = rest // sizes[name]
            peers.append((slots, peer))
            slots += 1
        phases.append(peers)
    for peers in phases:
        for _, peer in peers:
            pl.semaphore_signal(barrier, inc=1, device_id=peer, device_id_type=MESH)

    sub = lax.broadcasted_iota(jnp.int32, (SUB, ext_y), 0)
    lane = lax.broadcasted_iota(jnp.int32, (SUB, ext_y), 1)
    elem = lax.rem(sub, ext_x)

    def flag(yes):
        return jnp.where(yes, 1, 0)

    zero = jnp.float32(0.0)
    inside = {
        WEST: jnp.where((elem == 0) & (flag(has[WEST]) == 0), zero, lift),
        EAST: jnp.where((elem == ext_x - 1) & (flag(has[EAST]) == 0), zero, lift),
        SOUTH: jnp.where((sub >= ext_x) | ((lane == 0) & (flag(has[SOUTH]) == 0)), zero, lift),
        NORTH: jnp.where((sub < SUB - ext_x) | ((lane == ext_y - 1) & (flag(has[NORTH]) == 0)), zero, lift),
    }
    first_elem = (elem == 0) & (flag(has[WEST]) == 1)
    last_elem = (elem == ext_x - 1) & (flag(has[EAST]) == 1)
    first_lane = (lane == 0) & (flag(has[SOUTH]) == 1)
    last_lane = (lane == ext_y - 1) & (flag(has[NORTH]) == 1)

    def spread(rows):
        out = jnp.broadcast_to(rows[0:1], (SUB, ext_y))
        for e in range(1, ext_x):
            out = jnp.where(elem == e, jnp.broadcast_to(rows[e:e + 1], (SUB, ext_y)), out)
        return out

    for t, mat in enumerate((table, table.T)):
        for g in range(groups):
            for h in range(groups):
                for k in range(SUB // step):
                    column = jnp.zeros((SUB, ext_y), jnp.float32)
                    for r in range(SUB):
                        a = (SUB * g + r) // ext_x
                        b = (SUB * h + (r - k * step) % SUB) // ext_x
                        column = jnp.where(sub == r, jnp.float32(-mat[a, b]), column)
                    coef_y[t, g, h, k] = column
    for piece in arrive[:3]:
        piece.wait()
    for s in range(SECTIONS):
        wet_rows[s] = spread(wet_ref[s].astype(jnp.float32))
    zone = spread(zone_ref[...])
    rough = jnp.zeros((SUB, ext_y), jnp.float32)
    for z in range(ZONES):
        rough = jnp.where(zone == z, manning_ref[z], rough)
    rough_rows[...] = rough

    zone_acc[...] = jnp.zeros((SUB, ext_y), jnp.float32)

    def rows(g):
        return pl.ds(SUB * g, SUB)

    def roll(value, shift, axis):
        size = value.shape[axis]
        shift = shift % size
        return value if shift == 0 else pltpu.roll(value, shift, axis)

    def load_coef(t):
        return [[[coef_y[t, g, h, k] for k in range(per)] for h in range(groups)] for g in range(groups)]

    def minus_along_second(coef, source):
        turned = [[roll(source[h], k * step, 0) for k in range(per)] for h in range(groups)]
        return [
            sum(coef[g][h][k] * turned[h][k] for h in range(groups) for k in range(per))
            for g in range(groups)
        ]

    pair = n_ty == 2
    beyond = 1 - ty

    def copy(rnd, side, blk=None):
        if side in (EAST, WEST):
            source, there, sem, device = xs.at[rnd, side], xr.at[rnd, side], side, target[side]
        elif side is None:
            source, there = ys.at[rnd, ty, blk], yr.at[rnd, ty, blk]
            sem, device = 2 + blk, {"ty": beyond}
        else:
            source, there = ys.at[rnd, side - 2, blk], yr.at[rnd, side - 2, blk]
            sem, device = 2 + (side - 2) * blocks + blk, target[side]
        return pltpu.make_async_remote_copy(
            src_ref=source,
            dst_ref=there,
            send_sem=send_sem.at[rnd, sem],
            recv_sem=recv_sem.at[rnd, sem],
            device_id=device,
            device_id_type=MESH,
        )

    def start(rnd, sides, blk=None):
        if pair and NORTH in sides:
            copy(rnd, None, blk).start()
            return
        for side in sides:
            @pl.when(has[side])
            def _():
                copy(rnd, side, blk).start()

    def await_from(rnd, sides, blk=None):
        if pair and NORTH in sides:
            copy(rnd, None, blk).wait_recv()
            return
        for side in sides:
            @pl.when(has[opposite[side]])
            def _():
                copy(rnd, side, blk).wait_recv()

    def end_sends(rnd):
        for side in (EAST, WEST):
            @pl.when(has[side])
            def _():
                copy(rnd, side).wait_send()
        for blk in range(blocks):
            if pair:
                copy(rnd, None, blk).wait_send()
                continue
            for side in (NORTH, SOUTH):
                @pl.when(has[side])
                def _():
                    copy(rnd, side, blk).wait_send()

    def pack_x(rnd, c, east, west):
        to_east, to_west = east[0], west[0]
        for g in range(1, groups):
            to_east = jnp.where(elem == ext_x - 1 - g, roll(east[g], -g, 0), to_east)
            to_west = jnp.where(elem == g, roll(west[g], g, 0), to_west)
        xs[rnd, EAST, c] = to_east
        xs[rnd, WEST, c] = to_west

    def beside_x(rnd, c, g, east, west):
        from_west, from_east = xr[rnd, EAST, c], xr[rnd, WEST, c]
        at_west = jnp.where(first_elem, roll(from_west, -(ext_x - 1 - g), 0), roll(east[g], 1, 0))
        at_east = jnp.where(last_elem, roll(from_east, ext_x - 1 - g, 0), roll(west[g], -1, 0))
        return at_west, at_east

    slot_of = sub // ext_x

    def pack_y(rnd, c, blk, north, south):
        to_north, to_south = roll(north[0], ext_x, 0), south[0]
        for k in range(1, per):
            to_north = jnp.where(slot_of == k, roll(north[k], (k + 1) * ext_x, 0), to_north)
            to_south = jnp.where(slot_of == k, roll(south[k], k * ext_x, 0), to_south)
        ys[rnd, 0, blk, c] = roll(to_north, 1, 1)
        ys[rnd, 1, blk, c] = roll(to_south, -1, 1)

    def beside_y(rnd, c, i):
        blk, k = divmod(order.index(i), per)
        at_south = jnp.where(first_lane, yr[rnd, 0, blk, c], ys[rnd, 0, blk, c])
        at_north = jnp.where(last_lane, yr[rnd, 1, blk, c], ys[rnd, 1, blk, c])
        return roll(at_south, -k * ext_x, 0), roll(at_north, -(k + 1) * ext_x, 0)

    first, last = 0, groups - 1
    comps = range(3)
    pen = 0.5 * PENALTY_SPEED

    def put_fluxes(s, i):
        for g in range(groups):
            h, p, m = (state[s, c, i, rows(g)] for c in comps)
            ih = 1.0 / h
            u, v = p * ih, m * ih
            inv_h[s, i, rows(g)] = ih
            vel_x[s, i, rows(g)] = u
            vel_y[s, i, rows(g)] = v
            pressure = 0.5 * h * h
            cross = p * v
            fx = (p, p * u + pressure, cross)
            fy = (m, cross, m * v + pressure)
            for c in comps:
                flux_x[c, i, rows(g)] = fx[c]
                flux_y[c, i, rows(g)] = fy[c]
            if g == last:
                north = [0.5 * fy[c] + pen * q for c, q in enumerate((h, p, m))]
            if g == first:
                south = [pen * q - 0.5 * fy[c] for c, q in enumerate((h, p, m))]
        return north, south

    def run_columns(rnd, arrived, one_column, x_pack):
        faces = {}
        sweep = list(range(blocks))
        if arrived is not None:
            sweep = sweep[::-1]
        edge_sweep = [blk for blk in sweep if blk in edge_blocks]
        for blk in sweep:
            members = order[blk * per:(blk + 1) * per]
            inner = [i for i in members if i not in edge_i]
            edge = [i for i in members if i in edge_i]
            if arrived is not None:
                await_from(arrived, (NORTH, SOUTH), blk)
                for i in inner:
                    faces[i] = one_column(i)
                if blk == edge_sweep[0]:
                    await_from(arrived, (EAST, WEST))
            for i in edge:
                faces[i] = one_column(i)
            if rnd is not None and blk == edge_sweep[-1]:
                x_pack()
                start(rnd, (EAST, WEST))
            if arrived is None:
                for i in inner:
                    faces[i] = one_column(i)
            if rnd is not None:
                for c in comps:
                    pack_y(rnd, c, blk, [faces[i][0][c] for i in members], [faces[i][1][c] for i in members])
                start(rnd, (NORTH, SOUTH), blk)

    edge_blocks = sorted({order.index(i) // per for i in edge_i})

    def x_traces(s, c):
        east = [0.5 * flux_x[c, NP - 1, rows(g)] + pen * state[s, c, NP - 1, rows(g)] for g in range(groups)]
        west = [pen * state[s, c, 0, rows(g)] - 0.5 * flux_x[c, 0, rows(g)] for g in range(groups)]
        return east, west

    coefs = (0.5 * TIME_STEP, 0.5 * TIME_STEP, TIME_STEP)
    sums = (1.0, 2.0, 2.0, 1.0)
    final_weights = (TIME_STEP / 6.0, TIME_STEP / 3.0, TIME_STEP / 3.0, TIME_STEP / 6.0)

    def pack_forward(s):
        for c in comps:
            pack_x(s, c, *x_traces(s, c))

    def pack_back(rnd):
        for c in comps:
            pack_x(rnd, c, *cot_faces(c))

    def cot_faces(c):
        return (
            [acc[c, NP - 1, rows(g)] for g in range(groups)],
            [acc[c, 0, rows(g)] for g in range(groups)],
        )

    def set_up(i):
        state[0, 1, i] = mom_ref[0, i]
        state[0, 2, i] = mom_ref[1, i]
        return put_fluxes(0, i)

    for piece in arrive[3:]:
        piece.wait()
    pl.semaphore_wait(barrier, slots)
    run_columns(0, None, set_up, lambda: pack_forward(0))

    for s in range(SECTIONS):
        def volume(blk, _):
            coef = load_coef(0)
            rough_g = rough_rows[...]
            for n in range(per):
                i = blk * per + n
                out = [minus_along_second(coef, [flux_y[c, i, rows(g)] for g in range(groups)]) for c in comps]
                for g in range(groups):
                    h, p, m = (state[s, c, i, rows(g)] for c in comps)
                    u, v = vel_x[s, i, rows(g)], vel_y[s, i, rows(g)]
                    speed = jnp.sqrt(u * u + v * v + SPEED_FLOOR)
                    kr = rough_g * speed * jnp.exp((-4.0 / 3.0) * jnp.log(h))
                    drag_r[s, i, rows(g)] = kr
                    k = rough_g * kr
                    tend[0, i, rows(g)] = out[0][g]
                    tend[1, i, rows(g)] = out[1][g] - k * p
                    tend[2, i, rows(g)] = out[2][g] - k * m
            return _

        lax.fori_loop(0, blocks, volume, 0, unroll=True)

        def volume_x(c, _):
            for g in range(groups):
                out = along_first(table, [flux_x[c, i, rows(g)] for i in range(NP)])
                for i in range(NP):
                    tend[c, i, rows(g)] -= out[i]
            return _

        lax.fori_loop(0, 3, volume_x, 0, unroll=True)
        if s > 0:
            end_sends(s - 1)

        def finish(i):
            wet = wet_rows[s]
            for c in comps:
                at_south, at_north = beside_y(s, c, i)
                for g in range(groups):
                    slope = tend[c, i, rows(g)]
                    q = state[s, c, i, rows(g)]
                    if i in edge_i:
                        at_west, at_east = beside_x(s, c, g, *old_x[c])
                        if i == 0:
                            slope = slope + inside[WEST] * (at_west - (0.5 * flux_x[c, i, rows(g)] + pen * q))
                        else:
                            slope = slope + inside[EAST] * (at_east - (pen * q - 0.5 * flux_x[c, i, rows(g)]))
                    if g == first:
                        slope = slope + inside[SOUTH] * (at_south - (0.5 * flux_y[c, i, rows(g)] + pen * q))
                    if g == last:
                        slope = slope + inside[NORTH] * (at_north - (pen * q - 0.5 * flux_y[c, i, rows(g)]))
                    slope = wet * slope
                    start_q = state[0, c, i, rows(g)]
                    if s == 0:
                        acc[c, i, rows(g)] = slope
                    elif s < SECTIONS - 1:
                        acc[c, i, rows(g)] += sums[s] * slope
                    if s < SECTIONS - 1:
                        state[s + 1, c, i, rows(g)] = start_q + coefs[s] * slope
                    elif c > 0:
                        total = acc[c, i, rows(g)] + slope
                        final = start_q + (TIME_STEP / 6.0) * total
                        seed = weight_ref[i, rows(g)] * final
                        final_adj[c - 1, i, rows(g)] = seed
                        adj_ref[c, i, rows(g)] = seed
                    else:
                        adj_ref[c, i, rows(g)] = jnp.zeros((SUB, ext_y), jnp.float32)
            if s < SECTIONS - 1:
                return put_fluxes(s + 1, i)
            return put_cot(s, i)

        def put_cot(s, i):
            wet = wet_rows[s]
            north, south = [], []
            for c in comps:
                for g in range(groups):
                    value = None
                    if c > 0:
                        value = final_weights[s] * final_adj[c - 1, i, rows(g)]
                    if s < SECTIONS - 1:
                        back = coefs[s] * later[c, i, rows(g)]
                        value = back if value is None else value + back
                    if value is None:
                        value = jnp.zeros((SUB, ext_y), jnp.float32)
                    value = wet * value
                    acc[c, i, rows(g)] = value
                    if g == last:
                        north.append(value)
                    if g == first:
                        south.append(value)
            return north, south

        old_x = [x_traces(s, c) for c in comps]
        if s < SECTIONS - 1:
            run_columns(s + 1, s, finish, lambda: pack_forward(s + 1))
        else:
            run_columns(SECTIONS, s, finish, lambda: pack_back(SECTIONS))

    def zone_copy(n, slot, peer):
        return pltpu.make_async_remote_copy(
            src_ref=zs.at[n], dst_ref=zr.at[slot],
            send_sem=zsend_sem.at[slot], recv_sem=zrecv_sem.at[n],
            device_id=peer, device_id_type=MESH,
        )

    def zone_start(n):
        for slot, peer in phases[n]:
            zone_copy(n, slot, peer).start()

    def zone_end(n):
        if not phases[n]:
            return zs[n]
        part = zr.at[pl.ds(phases[n][0][0], len(phases[n]))]
        pltpu.make_async_copy(part, part, zrecv_sem.at[n]).wait()
        total = zs[n]
        for slot, _ in phases[n]:
            total = total + zr[slot]
        return total

    def write_out(n, c, first_i, count):
        part = pl.ds(first_i, count)
        return pltpu.make_async_copy(adj_ref.at[c, part], adj_hbm.at[c, part], out_sem.at[n, c])

    for s in reversed(range(SECTIONS)):
        rnd = 2 * SECTIONS - 1 - s
        def drag_back(blk, _):
            rough_g = rough_rows[...]
            parts = []
            for n in range(per):
                i = blk * per + n
                for g in range(groups):
                    h, p, m = (state[s, c, i, rows(g)] for c in comps)
                    u, v, ih = vel_x[s, i, rows(g)], vel_y[s, i, rows(g)], inv_h[s, i, rows(g)]
                    kr = drag_r[s, i, rows(g)]
                    c1, c2 = acc[1, i, rows(g)], acc[2, i, rows(g)]
                    part = kr * (c1 * p + c2 * m)
                    parts.append(part)
                    k = rough_g * kr
                    e = rough_g * part * ih
                    square = u * u + v * v
                    eq = e / (square + SPEED_FLOOR)
                    tend[0, i, rows(g)] = (4.0 / 3.0) * e + eq * square
                    tend[1, i, rows(g)] = -(k * c1 + eq * u)
                    tend[2, i, rows(g)] = -(k * c2 + eq * v)
            zone_acc[...] += sum(parts)
            return _

        lax.fori_loop(0, blocks, drag_back, 0, unroll=True)

        if s == 0:
            total = zone_acc[...]
            shift = ext_x
            while shift < SUB:
                total = total + roll(total, shift, 0)
                shift *= 2
            total = -2.0 * total
            zones = lax.broadcasted_iota(jnp.int32, (ZONES, ext_y), 0)
            spot = jnp.zeros((ZONES, ext_y), jnp.float32)
            for e in range(ext_x):
                ids = jnp.broadcast_to(zone_ref[e:e + 1, :], (ZONES, ext_y))
                spot = spot + jnp.where(ids == zones, jnp.broadcast_to(total[e:e + 1], (ZONES, ext_y)), 0.0)
            per_zone = jnp.sum(spot, axis=1, keepdims=True)
            spots = lax.broadcasted_iota(jnp.int32, (ZONES, ext_y), 1)
            line = jnp.sum(jnp.where(zones == spots, jnp.broadcast_to(per_zone, (ZONES, ext_y)), 0.0), axis=0, keepdims=True)
            zs[0] = line
            zone_start(0)

        def volume_y(blk, _):
            coef = load_coef(1)
            for n in range(per):
                i = blk * per + n
                for c in comps:
                    out = minus_along_second(coef, [acc[c, i, rows(g)] for g in range(groups)])
                    for g in range(groups):
                        flux_y[c, i, rows(g)] = out[g]
            return _

        lax.fori_loop(0, blocks, volume_y, 0, unroll=True)

        def volume_back(c, _):
            for g in range(groups):
                out = along_first(-table.T, [acc[c, i, rows(g)] for i in range(NP)])
                for i in range(NP):
                    flux_x[c, i, rows(g)] = out[i]
            return _

        lax.fori_loop(0, 3, volume_back, 0, unroll=True)
        end_sends(rnd - 1)

        old_x = [cot_faces(c) for c in comps]

        def finish_back(i):
            s_in, n_in, w_in, e_in = inside[SOUTH], inside[NORTH], inside[WEST], inside[EAST]
            beside = [beside_y(rnd, c, i) for c in comps]
            for g in range(groups):
                a = [flux_x[c, i, rows(g)] for c in comps]
                b = [flux_y[c, i, rows(g)] for c in comps]
                out = [tend[c, i, rows(g)] for c in comps]
                own = [acc[c, i, rows(g)] for c in comps]
                for c in comps:
                    if i in edge_i:
                        at_west, at_east = beside_x(rnd, c, g, *old_x[c])
                        if i == 0:
                            a[c] = a[c] - (0.5 * w_in) * (own[c] + at_west)
                            out[c] = out[c] + (pen * w_in) * (at_west - own[c])
                        else:
                            a[c] = a[c] + (0.5 * e_in) * (own[c] + at_east)
                            out[c] = out[c] + (pen * e_in) * (at_east - own[c])
                    if g == first:
                        there = beside[c][0]
                        b[c] = b[c] - (0.5 * s_in) * (own[c] + there)
                        out[c] = out[c] + (pen * s_in) * (there - own[c])
                    if g == last:
                        there = beside[c][1]
                        b[c] = b[c] + (0.5 * n_in) * (own[c] + there)
                        out[c] = out[c] + (pen * n_in) * (there - own[c])
                h = state[s, 0, i, rows(g)]
                u, v = vel_x[s, i, rows(g)], vel_y[s, i, rows(g)]
                cross = a[2] + b[1]
                au, bv = a[1] * u, b[2] * v
                cot = (
                    out[0] + (a[1] + b[2]) * h - au * u - bv * v - cross * (u * v),
                    out[1] + a[0] + 2.0 * au + cross * v,
                    out[2] + b[0] + 2.0 * bv + cross * u,
                )
                for c in comps:
                    adj_ref[c, i, rows(g)] += cot[c]
                    if s > 0:
                        later[c, i, rows(g)] = cot[c]
            if s > 0:
                return put_cot(s - 1, i)

        if s > 0:
            run_columns(rnd + 1, rnd, finish_back, lambda: pack_back(rnd + 1))
        else:
            run_columns(None, rnd, finish_back, None)

    writes = [write_out(0, c, 0, NP) for c in comps]
    for write in writes:
        write.start()
    whole = zone_end(0)
    if not direct:
        zs[1] = whole
        zone_start(1)
        whole = zone_end(1)
    nodes = events * n_ev * ext_x * n_tx * ext_y * n_ty * NP * NP
    grad_ref[...] = whole[:, :ZONES] * (ZONES / (TIME_STEP * nodes))

    end_sends(2 * SECTIONS - 1)
    for n, peers in enumerate(phases):
        for slot, peer in peers:
            zone_copy(n, slot, peer).wait_send()
    for write in writes:
        write.wait()


def hand_over(adjoint_ref, grad_ref, adjoint_out, grad_out, sem):
    moves = [pltpu.make_async_copy(adjoint_ref.at[c], adjoint_out.at[c], sem.at[c]) for c in range(3)]
    moves.append(pltpu.make_async_copy(grad_ref, grad_out, sem.at[3]))
    for move in moves:
        move.start()
    for move in moves:
        move.wait()


def local(axes, depth0, momentum0, obs_weight, wet_mask, zone_id, manning):
    ext_x, ext_y = depth0.shape[3:]
    rows = NP * ext_x
    field = (NP, rows, ext_y)
    rounds = 2 * SECTIONS
    slots = axes["ty"] * axes["ev"] * axes["tx"]
    if slots > DIRECT:
        slots = axes["ty"] * axes["ev"] + axes["tx"]
    f32 = jnp.float32
    vmem = pl.BlockSpec(memory_space=pltpu.VMEM)
    adjoint, grad = pl.pallas_call(
        functools.partial(kernel, axes, ext_x, depth0.shape[0]),
        out_shape=(
            jax.ShapeDtypeStruct((3,) + field, f32),
            jax.ShapeDtypeStruct((1, ZONES), f32),
        ),
        in_specs=[pl.BlockSpec(memory_space=pltpu.HBM)] * 6,
        out_specs=(pl.BlockSpec(memory_space=pltpu.HBM), vmem),
        scratch_shapes=[
            pltpu.VMEM((3,) + field, f32),
            pltpu.SemaphoreType.DMA((1, 3)),
            pltpu.VMEM((2,) + field, f32),
            pltpu.VMEM(field, f32),
            pltpu.VMEM(wet_mask.shape[1:], jnp.int32),
            pltpu.VMEM(zone_id.shape, jnp.int32),
            pltpu.SMEM(manning.shape, f32),
            pltpu.SemaphoreType.DMA((6,)),
            pltpu.VMEM((SECTIONS, 3) + field, f32),
            pltpu.VMEM((SECTIONS,) + field, f32),
            pltpu.VMEM((SECTIONS,) + field, f32),
            pltpu.VMEM((SECTIONS,) + field, f32),
            pltpu.VMEM((SECTIONS,) + field, f32),
            pltpu.VMEM((3,) + field, f32),
            pltpu.VMEM((3,) + field, f32),
            pltpu.VMEM((3,) + field, f32),
            pltpu.VMEM((3,) + field, f32),
            pltpu.VMEM((2,) + field, f32),
            pltpu.VMEM((3,) + field, f32),
            pltpu.VMEM((SECTIONS, SUB, ext_y), f32),
            pltpu.VMEM((SUB, ext_y), f32),
            pltpu.VMEM((2, ext_x, ext_x, SUB // ext_x, SUB, ext_y), f32),
            pltpu.VMEM((SUB, ext_y), f32),
            pltpu.VMEM((rounds, 2, 3, SUB, ext_y), f32),
            pltpu.VMEM((rounds, 2, 3, SUB, ext_y), f32),
            pltpu.VMEM((rounds, 2, NP // (SUB // ext_x), 3, SUB, ext_y), f32),
            pltpu.VMEM((rounds, 2, NP // (SUB // ext_x), 3, SUB, ext_y), f32),
            pltpu.VMEM((2, 1, ext_y), f32),
            pltpu.VMEM((slots, 1, ext_y), f32),
            pltpu.SemaphoreType.DMA((rounds, 2 + 2 * (NP // (SUB // ext_x)))),
            pltpu.SemaphoreType.DMA((rounds, 2 + 2 * (NP // (SUB // ext_x)))),
            pltpu.SemaphoreType.DMA((slots,)),
            pltpu.SemaphoreType.DMA((slots,)),
        ],
        compiler_params=pltpu.CompilerParams(
            collective_id=0, has_side_effects=True, vmem_limit_bytes=60 * 1024 * 1024
        ),
    )(
        depth0.reshape(field),
        momentum0.reshape((2,) + field),
        obs_weight.reshape(field),
        wet_mask.reshape(wet_mask.shape[1:]),
        zone_id,
        manning,
    )
    anywhere = pl.BlockSpec(memory_space=pl.ANY)
    adjoint, grad = pl.pallas_call(
        hand_over,
        out_shape=(
            jax.ShapeDtypeStruct(adjoint.shape, f32),
            jax.ShapeDtypeStruct(grad.shape, f32),
        ),
        in_specs=[anywhere] * 2,
        out_specs=(anywhere, anywhere),
        scratch_shapes=[pltpu.SemaphoreType.DMA((4,))],
    )(adjoint, grad)
    return adjoint.reshape((1, 3, NP, NP, ext_x, ext_y)), grad.reshape((ZONES,))


def solution(mesh):
    in_specs = (
        P(("basin", "ev"), None, None, "tx", "ty"),
        P(("basin", "ev"), None, None, None, "tx", "ty"),
        P(("basin", "ev"), None, None, "tx", "ty"),
        P(("basin", "ev"), None, "tx", "ty"),
        P(("basin", "tx"), "ty"),
        P("basin"),
    )
    out_specs = (P(("basin", "ev"), None, None, None, "tx", "ty"), P("basin"))
    return jax.shard_map(
        functools.partial(local, dict(mesh.shape)),
        mesh=mesh, in_specs=in_specs, out_specs=out_specs, check_vma=False,
    )
```

```python
import functools

import jax
import jax.numpy as jnp
import numpy as np
from jax import lax
from jax.experimental import pallas as pl
from jax.experimental.pallas import tpu as pltpu
from jax.sharding import PartitionSpec as P

NP = 8
SECTIONS = 4
ZONES = 32
SUB = 8

PENALTY_SPEED = 4.0
TIME_STEP = 0.0005
SPEED_FLOOR = 0.01
MESH = pl.DeviceIdType.MESH
EAST, WEST, NORTH, SOUTH = range(4)
DIRECT = 32


def node_tables():
    points = -np.cos(np.pi * np.arange(NP) / (NP - 1))
    identity = np.eye(NP)
    differ = points[:, None] - points[None, :] + identity
    barycentric = 1.0 / np.prod(differ, axis=1)
    derivative = barycentric[None, :] / barycentric[:, None] / differ * (1.0 - identity)
    derivative = derivative - identity * derivative.sum(axis=1)[:, None]
    order = NP - 1
    end_weight = 1.0 / (order * order)
    return (derivative, float(1.0 / end_weight))


def along_first(table, slabs):
    half = NP // 2
    even = [slabs[k] + slabs[NP - 1 - k] for k in range(half)]
    odd = [slabs[k] - slabs[NP - 1 - k] for k in range(half)]
    out = [None] * NP
    for a in range(half):
        on_even = sum(float(0.5 * (table[a, k] + table[a, NP - 1 - k])) * even[k] for k in range(half))
        on_odd = sum(float(0.5 * (table[a, k] - table[a, NP - 1 - k])) * odd[k] for k in range(half))
        out[a] = on_odd + on_even
        out[NP - 1 - a] = on_odd - on_even
    return out


def kernel(
    axes, ext_x, events,
    depth_hbm, mom_hbm, weight_hbm, wet_hbm, zone_hbm, manning_hbm,
    adj_hbm, grad_ref,
    adj_ref, out_sem, mom_ref, weight_ref, wet_ref, zone_ref, manning_ref, in_sem,
    state, vel_x, vel_y, inv_h, drag_r, flux_x, flux_y, tend, acc, final_adj, later,
    wet_rows, rough_rows, coef_y, zone_acc,
    xs, xr, ys, yr, zs, zr, send_sem, recv_sem, zsend_sem, zrecv_sem,
):
    table, lift = node_tables()
    n_tx, n_ty, n_ev = axes["tx"], axes["ty"], axes["ev"]
    tx, ty, ev = lax.axis_index("tx"), lax.axis_index("ty"), lax.axis_index("ev")
    ext_y = depth_hbm.shape[-1]
    groups = ext_x
    step = ext_x
    per = SUB // ext_x
    edge_i = (0, NP - 1)
    inner_i = tuple(range(1, NP - 1))
    blocks = NP // per
    packs = []
    spans = []
    for members in (edge_i, inner_i):
        first_pack = len(packs)
        packs += [members[n:n + per] for n in range(0, len(members), per)]
        spans.append((first_pack, len(packs) - first_pack))
    parts = len(spans)
    has = {EAST: tx < n_tx - 1, WEST: tx > 0, NORTH: ty < n_ty - 1, SOUTH: ty > 0}
    target = {EAST: {"tx": tx + 1}, WEST: {"tx": tx - 1}, NORTH: {"ty": ty + 1}, SOUTH: {"ty": ty - 1}}
    opposite = {EAST: WEST, WEST: EAST, NORTH: SOUTH, SOUTH: NORTH}

    arrive = [
        pltpu.make_async_copy(source, target_ref, in_sem.at[n])
        for n, (source, target_ref) in enumerate((
            (zone_hbm, zone_ref), (manning_hbm, manning_ref), (wet_hbm, wet_ref),
            (depth_hbm, state.at[0, 0]), (mom_hbm, mom_ref), (weight_hbm, weight_ref),
        ))
    ]
    for piece in arrive:
        piece.start()

    barrier = pltpu.get_barrier_semaphore()
    sizes = {"ty": n_ty, "ev": n_ev, "tx": n_tx}
    all_names = ("ty", "ev", "tx")
    direct = n_ty * n_ev * n_tx <= DIRECT
    phases = []
    slots = 0
    for names in ((all_names,) if direct else (all_names[:2], all_names[2:])):
        count = int(np.prod([sizes[name] for name in names]))
        here = 0
        for name in names:
            here = here * sizes[name] + lax.axis_index(name)
        peers = []
        for k in range(1, count):
            rest = lax.rem(here + k, count)
            peer = {}
            for name in reversed(names):
                peer[name] = lax.rem(rest, sizes[name])
                rest = rest // sizes[name]
            peers.append((slots, peer))
            slots += 1
        phases.append(peers)
    for peers in phases:
        for _, peer in peers:
            pl.semaphore_signal(barrier, inc=1, device_id=peer, device_id_type=MESH)

    sub = lax.broadcasted_iota(jnp.int32, (SUB, ext_y), 0)
    lane = lax.broadcasted_iota(jnp.int32, (SUB, ext_y), 1)
    elem = lax.rem(sub, ext_x)

    def flag(yes):
        return jnp.where(yes, 1, 0)

    zero = jnp.float32(0.0)
    inside = {
        WEST: jnp.where((elem == 0) & (flag(has[WEST]) == 0), zero, lift),
        EAST: jnp.where((elem == ext_x - 1) & (flag(has[EAST]) == 0), zero, lift),
        SOUTH: jnp.where((sub >= ext_x) | ((lane == 0) & (flag(has[SOUTH]) == 0)), zero, lift),
        NORTH: jnp.where((sub < SUB - ext_x) | ((lane == ext_y - 1) & (flag(has[NORTH]) == 0)), zero, lift),
    }
    first_elem = (elem == 0) & (flag(has[WEST]) == 1)
    last_elem = (elem == ext_x - 1) & (flag(has[EAST]) == 1)
    first_lane = (lane == 0) & (flag(has[SOUTH]) == 1)
    last_lane = (lane == ext_y - 1) & (flag(has[NORTH]) == 1)

    def spread(rows):
        out = jnp.broadcast_to(rows[0:1], (SUB, ext_y))
        for e in range(1, ext_x):
            out = jnp.where(elem == e, jnp.broadcast_to(rows[e:e + 1], (SUB, ext_y)), out)
        return out

    for t, mat in enumerate((table, table.T)):
        for g in range(groups):
            for h in range(groups):
                for k in range(SUB // step):
                    column = jnp.zeros((SUB, ext_y), jnp.float32)
                    for r in range(SUB):
                        a = (SUB * g + r) // ext_x
                        b = (SUB * h + (r - k * step) % SUB) // ext_x
                        column = jnp.where(sub == r, jnp.float32(-mat[a, b]), column)
                    coef_y[t, g, h, k] = column
    for piece in arrive[:3]:
        piece.wait()
    for s in range(SECTIONS):
        wet_rows[s] = spread(wet_ref[s].astype(jnp.float32))
    zone = spread(zone_ref[...])
    rough = jnp.zeros((SUB, ext_y), jnp.float32)
    for z in range(ZONES):
        rough = jnp.where(zone == z, manning_ref[z], rough)
    rough_rows[...] = rough

    zone_acc[...] = jnp.zeros((SUB, ext_y), jnp.float32)

    def rows(g):
        return pl.ds(SUB * g, SUB)

    def roll(value, shift, axis):
        size = value.shape[axis]
        shift = shift % size
        return value if shift == 0 else pltpu.roll(value, shift, axis)

    def load_coef(t):
        return [[[coef_y[t, g, h, k] for k in range(per)] for h in range(groups)] for g in range(groups)]

    def minus_along_second(coef, source):
        turned = [[roll(source[h], k * step, 0) for k in range(per)] for h in range(groups)]
        return [
            sum(coef[g][h][k] * turned[h][k] for h in range(groups) for k in range(per))
            for g in range(groups)
        ]

    pair = n_ty == 2
    beyond = 1 - ty

    def copy(rnd, side, blk=None):
        if side in (EAST, WEST):
            source, there, sem, device = xs.at[rnd, side], xr.at[rnd, side], side, target[side]
        elif side is None:
            span = pl.ds(*spans[blk])
            source, there = ys.at[rnd, ty, span], yr.at[rnd, ty, span]
            sem, device = 2 + blk, {"ty": beyond}
        else:
            span = pl.ds(*spans[blk])
            source, there = ys.at[rnd, side - 2, span], yr.at[rnd, side - 2, span]
            sem, device = 2 + (side - 2) * parts + blk, target[side]
        return pltpu.make_async_remote_copy(
            src_ref=source,
            dst_ref=there,
            send_sem=send_sem.at[rnd, sem],
            recv_sem=recv_sem.at[rnd, sem],
            device_id=device,
            device_id_type=MESH,
        )

    def start(rnd, sides, blk=None):
        if pair and NORTH in sides:
            copy(rnd, None, blk).start()
            return
        for side in sides:
            @pl.when(has[side])
            def _():
                copy(rnd, side, blk).start()

    def await_from(rnd, sides, blk=None):
        if pair and NORTH in sides:
            copy(rnd, None, blk).wait_recv()
            return
        for side in sides:
            @pl.when(has[opposite[side]])
            def _():
                copy(rnd, side, blk).wait_recv()

    def end_sends(rnd):
        for side in (EAST, WEST):
            @pl.when(has[side])
            def _():
                copy(rnd, side).wait_send()
        for blk in range(parts):
            if pair:
                copy(rnd, None, blk).wait_send()
                continue
            for side in (NORTH, SOUTH):
                @pl.when(has[side])
                def _():
                    copy(rnd, side, blk).wait_send()

    def pack_x(rnd, c, east, west):
        to_east, to_west = east[0], west[0]
        for g in range(1, groups):
            to_east = jnp.where(elem == ext_x - 1 - g, roll(east[g], -g, 0), to_east)
            to_west = jnp.where(elem == g, roll(west[g], g, 0), to_west)
        xs[rnd, EAST, c] = to_east
        xs[rnd, WEST, c] = to_west

    def beside_x(rnd, c, g, east, west):
        from_west, from_east = xr[rnd, EAST, c], xr[rnd, WEST, c]
        at_west = jnp.where(first_elem, roll(from_west, -(ext_x - 1 - g), 0), roll(east[g], 1, 0))
        at_east = jnp.where(last_elem, roll(from_east, ext_x - 1 - g, 0), roll(west[g], -1, 0))
        return at_west, at_east

    slot_of = sub // ext_x

    def pack_y(rnd, c, blk, north, south):
        to_north, to_south = roll(north[0], ext_x, 0), south[0]
        for k in range(1, len(north)):
            to_north = jnp.where(slot_of == k, roll(north[k], (k + 1) * ext_x, 0), to_north)
            to_south = jnp.where(slot_of == k, roll(south[k], k * ext_x, 0), to_south)
        ys[rnd, 0, blk, c] = roll(to_north, 1, 1)
        ys[rnd, 1, blk, c] = roll(to_south, -1, 1)

    def beside_y(rnd, c, i):
        blk, k = next((n, m.index(i)) for n, m in enumerate(packs) if i in m)
        at_south = jnp.where(first_lane, yr[rnd, 0, blk, c], ys[rnd, 0, blk, c])
        at_north = jnp.where(last_lane, yr[rnd, 1, blk, c], ys[rnd, 1, blk, c])
        return roll(at_south, -k * ext_x, 0), roll(at_north, -(k + 1) * ext_x, 0)

    first, last = 0, groups - 1
    comps = range(3)
    pen = 0.5 * PENALTY_SPEED

    def put_fluxes(s, i):
        for g in range(groups):
            h, p, m = (state[s, c, i, rows(g)] for c in comps)
            ih = 1.0 / h
            u, v = p * ih, m * ih
            inv_h[s, i, rows(g)] = ih
            vel_x[s, i, rows(g)] = u
            vel_y[s, i, rows(g)] = v
            pressure = 0.5 * h * h
            cross = p * v
            fx = (p, p * u + pressure, cross)
            fy = (m, cross, m * v + pressure)
            for c in comps:
                flux_x[c, i, rows(g)] = fx[c]
                flux_y[c, i, rows(g)] = fy[c]
            if g == last:
                north = [0.5 * fy[c] + pen * q for c, q in enumerate((h, p, m))]
            if g == first:
                south = [pen * q - 0.5 * fy[c] for c, q in enumerate((h, p, m))]
        return north, south

    def run_columns(rnd, arrived, one_column, x_pack):
        for part in ((0, 1) if arrived is None else (1, 0)):
            if arrived is not None:
                await_from(arrived, (NORTH, SOUTH), part)
                if part == 0:
                    await_from(arrived, (EAST, WEST))
            faces = {i: one_column(i) for i in (edge_i, inner_i)[part]}
            if rnd is None:
                continue
            if part == 0:
                x_pack()
                start(rnd, (EAST, WEST))
            head, count = spans[part]
            for blk in range(head, head + count):
                for c in comps:
                    pack_y(rnd, c, blk, [faces[i][0][c] for i in packs[blk]], [faces[i][1][c] for i in packs[blk]])
            start(rnd, (NORTH, SOUTH), part)

    def x_traces(s, c):
        east = [0.5 * flux_x[c, NP - 1, rows(g)] + pen * state[s, c, NP - 1, rows(g)] for g in range(groups)]
        west = [pen * state[s, c, 0, rows(g)] - 0.5 * flux_x[c, 0, rows(g)] for g in range(groups)]
        return east, west

    coefs = (0.5 * TIME_STEP, 0.5 * TIME_STEP, TIME_STEP)
    sums = (1.0, 2.0, 2.0, 1.0)
    final_weights = (TIME_STEP / 6.0, TIME_STEP / 3.0, TIME_STEP / 3.0, TIME_STEP / 6.0)

    def pack_forward(s):
        for c in comps:
            pack_x(s, c, *x_traces(s, c))

    def pack_back(rnd):
        for c in comps:
            pack_x(rnd, c, *cot_faces(c))

    def cot_faces(c):
        return (
            [acc[c, NP - 1, rows(g)] for g in range(groups)],
            [acc[c, 0, rows(g)] for g in range(groups)],
        )

    def set_up(i):
        state[0, 1, i] = mom_ref[0, i]
        state[0, 2, i] = mom_ref[1, i]
        return put_fluxes(0, i)

    for piece in arrive[3:]:
        piece.wait()
    pl.semaphore_wait(barrier, slots)
    run_columns(0, None, set_up, lambda: pack_forward(0))

    for s in range(SECTIONS):
        def volume(blk, _):
            coef = load_coef(0)
            rough_g = rough_rows[...]
            for n in range(per):
                i = blk * per + n
                out = [minus_along_second(coef, [flux_y[c, i, rows(g)] for g in range(groups)]) for c in comps]
                for g in range(groups):
                    h, p, m = (state[s, c, i, rows(g)] for c in comps)
                    u, v = vel_x[s, i, rows(g)], vel_y[s, i, rows(g)]
                    speed = jnp.sqrt(u * u + v * v + SPEED_FLOOR)
                    kr = rough_g * speed * jnp.exp((-4.0 / 3.0) * jnp.log(h))
                    drag_r[s, i, rows(g)] = kr
                    k = rough_g * kr
                    tend[0, i, rows(g)] = out[0][g]
                    tend[1, i, rows(g)] = out[1][g] - k * p
                    tend[2, i, rows(g)] = out[2][g] - k * m
            return _

        lax.fori_loop(0, blocks, volume, 0, unroll=True)

        def volume_x(c, _):
            for g in range(groups):
                out = along_first(table, [flux_x[c, i, rows(g)] for i in range(NP)])
                for i in range(NP):
                    tend[c, i, rows(g)] -= out[i]
            return _

        lax.fori_loop(0, 3, volume_x, 0, unroll=True)
        if s > 0:
            end_sends(s - 1)

        def finish(i):
            wet = wet_rows[s]
            for c in comps:
                at_south, at_north = beside_y(s, c, i)
                for g in range(groups):
                    slope = tend[c, i, rows(g)]
                    q = state[s, c, i, rows(g)]
                    if i in edge_i:
                        at_west, at_east = beside_x(s, c, g, *old_x[c])
                        if i == 0:
                            slope = slope + inside[WEST] * (at_west - (0.5 * flux_x[c, i, rows(g)] + pen * q))
                        else:
                            slope = slope + inside[EAST] * (at_east - (pen * q - 0.5 * flux_x[c, i, rows(g)]))
                    if g == first:
                        slope = slope + inside[SOUTH] * (at_south - (0.5 * flux_y[c, i, rows(g)] + pen * q))
                    if g == last:
                        slope = slope + inside[NORTH] * (at_north - (pen * q - 0.5 * flux_y[c, i, rows(g)]))
                    slope = wet * slope
                    start_q = state[0, c, i, rows(g)]
                    if s == 0:
                        acc[c, i, rows(g)] = slope
                    elif s < SECTIONS - 1:
                        acc[c, i, rows(g)] += sums[s] * slope
                    if s < SECTIONS - 1:
                        state[s + 1, c, i, rows(g)] = start_q + coefs[s] * slope
                    elif c > 0:
                        total = acc[c, i, rows(g)] + slope
                        final = start_q + (TIME_STEP / 6.0) * total
                        seed = weight_ref[i, rows(g)] * final
                        final_adj[c - 1, i, rows(g)] = seed
                        adj_ref[c, i, rows(g)] = seed
                    else:
                        adj_ref[c, i, rows(g)] = jnp.zeros((SUB, ext_y), jnp.float32)
            if s < SECTIONS - 1:
                return put_fluxes(s + 1, i)
            return put_cot(s, i)

        def put_cot(s, i):
            wet = wet_rows[s]
            north, south = [], []
            for c in comps:
                for g in range(groups):
                    value = None
                    if c > 0:
                        value = final_weights[s] * final_adj[c - 1, i, rows(g)]
                    if s < SECTIONS - 1:
                        back = coefs[s] * later[c, i, rows(g)]
                        value = back if value is None else value + back
                    if value is None:
                        value = jnp.zeros((SUB, ext_y), jnp.float32)
                    value = wet * value
                    acc[c, i, rows(g)] = value
                    if g == last:
                        north.append(value)
                    if g == first:
                        south.append(value)
            return north, south

        old_x = [x_traces(s, c) for c in comps]
        if s < SECTIONS - 1:
            run_columns(s + 1, s, finish, lambda: pack_forward(s + 1))
        else:
            run_columns(SECTIONS, s, finish, lambda: pack_back(SECTIONS))

    def zone_copy(n, slot, peer):
        return pltpu.make_async_remote_copy(
            src_ref=zs.at[n], dst_ref=zr.at[slot],
            send_sem=zsend_sem.at[slot], recv_sem=zrecv_sem.at[n],
            device_id=peer, device_id_type=MESH,
        )

    def zone_start(n):
        for slot, peer in phases[n]:
            zone_copy(n, slot, peer).start()

    def zone_end(n):
        if not phases[n]:
            return zs[n]
        part = zr.at[pl.ds(phases[n][0][0], len(phases[n]))]
        pltpu.make_async_copy(part, part, zrecv_sem.at[n]).wait()
        total = zs[n]
        for slot, _ in phases[n]:
            total = total + zr[slot]
        return total

    def write_out(n, c, first_i, count):
        part = pl.ds(first_i, count)
        return pltpu.make_async_copy(adj_ref.at[c, part], adj_hbm.at[c, part], out_sem.at[n, c])

    for s in reversed(range(SECTIONS)):
        rnd = 2 * SECTIONS - 1 - s
        def drag_back(blk, _):
            rough_g = rough_rows[...]
            parts = []
            for n in range(per):
                i = blk * per + n
                for g in range(groups):
                    h, p, m = (state[s, c, i, rows(g)] for c in comps)
                    u, v, ih = vel_x[s, i, rows(g)], vel_y[s, i, rows(g)], inv_h[s, i, rows(g)]
                    kr = drag_r[s, i, rows(g)]
                    c1, c2 = acc[1, i, rows(g)], acc[2, i, rows(g)]
                    part = kr * (c1 * p + c2 * m)
                    parts.append(part)
                    k = rough_g * kr
                    e = rough_g * part * ih
                    square = u * u + v * v
                    eq = e / (square + SPEED_FLOOR)
                    tend[0, i, rows(g)] = (4.0 / 3.0) * e + eq * square
                    tend[1, i, rows(g)] = -(k * c1 + eq * u)
                    tend[2, i, rows(g)] = -(k * c2 + eq * v)
            zone_acc[...] += sum(parts)
            return _

        lax.fori_loop(0, blocks, drag_back, 0, unroll=True)

        if s == 0:
            total = zone_acc[...]
            shift = ext_x
            while shift < SUB:
                total = total + roll(total, shift, 0)
                shift *= 2
            total = -2.0 * total
            zones = lax.broadcasted_iota(jnp.int32, (ZONES, ext_y), 0)
            spot = jnp.zeros((ZONES, ext_y), jnp.float32)
            for e in range(ext_x):
                ids = jnp.broadcast_to(zone_ref[e:e + 1, :], (ZONES, ext_y))
                spot = spot + jnp.where(ids == zones, jnp.broadcast_to(total[e:e + 1], (ZONES, ext_y)), 0.0)
            per_zone = jnp.sum(spot, axis=1, keepdims=True)
            spots = lax.broadcasted_iota(jnp.int32, (ZONES, ext_y), 1)
            line = jnp.sum(jnp.where(zones == spots, jnp.broadcast_to(per_zone, (ZONES, ext_y)), 0.0), axis=0, keepdims=True)
            zs[0] = line
            zone_start(0)

        def volume_y(blk, _):
            coef = load_coef(1)
            for n in range(per):
                i = blk * per + n
                for c in comps:
                    out = minus_along_second(coef, [acc[c, i, rows(g)] for g in range(groups)])
                    for g in range(groups):
                        flux_y[c, i, rows(g)] = out[g]
            return _

        lax.fori_loop(0, blocks, volume_y, 0, unroll=True)

        def volume_back(c, _):
            for g in range(groups):
                out = along_first(-table.T, [acc[c, i, rows(g)] for i in range(NP)])
                for i in range(NP):
                    flux_x[c, i, rows(g)] = out[i]
            return _

        lax.fori_loop(0, 3, volume_back, 0, unroll=True)
        end_sends(rnd - 1)

        old_x = [cot_faces(c) for c in comps]

        def finish_back(i):
            s_in, n_in, w_in, e_in = inside[SOUTH], inside[NORTH], inside[WEST], inside[EAST]
            beside = [beside_y(rnd, c, i) for c in comps]
            for g in range(groups):
                a = [flux_x[c, i, rows(g)] for c in comps]
                b = [flux_y[c, i, rows(g)] for c in comps]
                out = [tend[c, i, rows(g)] for c in comps]
                own = [acc[c, i, rows(g)] for c in comps]
                for c in comps:
                    if i in edge_i:
                        at_west, at_east = beside_x(rnd, c, g, *old_x[c])
                        if i == 0:
                            a[c] = a[c] - (0.5 * w_in) * (own[c] + at_west)
                            out[c] = out[c] + (pen * w_in) * (at_west - own[c])
                        else:
                            a[c] = a[c] + (0.5 * e_in) * (own[c] + at_east)
                            out[c] = out[c] + (pen * e_in) * (at_east - own[c])
                    if g == first:
                        there = beside[c][0]
                        b[c] = b[c] - (0.5 * s_in) * (own[c] + there)
                        out[c] = out[c] + (pen * s_in) * (there - own[c])
                    if g == last:
                        there = beside[c][1]
                        b[c] = b[c] + (0.5 * n_in) * (own[c] + there)
                        out[c] = out[c] + (pen * n_in) * (there - own[c])
                h = state[s, 0, i, rows(g)]
                u, v = vel_x[s, i, rows(g)], vel_y[s, i, rows(g)]
                cross = a[2] + b[1]
                au, bv = a[1] * u, b[2] * v
                cot = (
                    out[0] + (a[1] + b[2]) * h - au * u - bv * v - cross * (u * v),
                    out[1] + a[0] + 2.0 * au + cross * v,
                    out[2] + b[0] + 2.0 * bv + cross * u,
                )
                for c in comps:
                    adj_ref[c, i, rows(g)] += cot[c]
                    if s > 0:
                        later[c, i, rows(g)] = cot[c]
            if s > 0:
                return put_cot(s - 1, i)

        if s > 0:
            run_columns(rnd + 1, rnd, finish_back, lambda: pack_back(rnd + 1))
        else:
            run_columns(None, rnd, finish_back, None)

    writes = [write_out(0, c, 0, NP) for c in comps]
    for write in writes:
        write.start()
    whole = zone_end(0)
    if not direct:
        zs[1] = whole
        zone_start(1)
        whole = zone_end(1)
    nodes = events * n_ev * ext_x * n_tx * ext_y * n_ty * NP * NP
    grad_ref[...] = whole[:, :ZONES] * (ZONES / (TIME_STEP * nodes))

    end_sends(2 * SECTIONS - 1)
    for n, peers in enumerate(phases):
        for slot, peer in peers:
            zone_copy(n, slot, peer).wait_send()
    for write in writes:
        write.wait()


def hand_over(adjoint_ref, grad_ref, adjoint_out, grad_out, adjoint_mid, grad_mid, sem):
    take = [pltpu.make_async_copy(adjoint_ref.at[c], adjoint_mid.at[c], sem.at[c]) for c in range(3)]
    give = [pltpu.make_async_copy(adjoint_mid.at[c], adjoint_out.at[c], sem.at[4 + c]) for c in range(3)]
    take.append(pltpu.make_async_copy(grad_ref, grad_mid, sem.at[3]))
    give.append(pltpu.make_async_copy(grad_mid, grad_out, sem.at[7]))
    for move in take:
        move.start()
    for taken, given in zip(take, give):
        taken.wait()
        given.start()
    for move in give:
        move.wait()


def local(axes, depth0, momentum0, obs_weight, wet_mask, zone_id, manning):
    ext_x, ext_y = depth0.shape[3:]
    rows = NP * ext_x
    field = (NP, rows, ext_y)
    rounds = 2 * SECTIONS
    packs = pl.cdiv(2 * ext_x, SUB) + pl.cdiv((NP - 2) * ext_x, SUB)
    slots = axes["ty"] * axes["ev"] * axes["tx"]
    if slots > DIRECT:
        slots = axes["ty"] * axes["ev"] + axes["tx"]
    f32 = jnp.float32
    vmem = pl.BlockSpec(memory_space=pltpu.VMEM)
    adjoint, grad = pl.pallas_call(
        functools.partial(kernel, axes, ext_x, depth0.shape[0]),
        out_shape=(
            jax.ShapeDtypeStruct((3,) + field, f32),
            jax.ShapeDtypeStruct((1, ZONES), f32),
        ),
        in_specs=[pl.BlockSpec(memory_space=pltpu.HBM)] * 6,
        out_specs=(pl.BlockSpec(memory_space=pltpu.HBM), vmem),
        scratch_shapes=[
            pltpu.VMEM((3,) + field, f32),
            pltpu.SemaphoreType.DMA((1, 3)),
            pltpu.VMEM((2,) + field, f32),
            pltpu.VMEM(field, f32),
            pltpu.VMEM(wet_mask.shape[1:], jnp.int32),
            pltpu.VMEM(zone_id.shape, jnp.int32),
            pltpu.SMEM(manning.shape, f32),
            pltpu.SemaphoreType.DMA((6,)),
            pltpu.VMEM((SECTIONS, 3) + field, f32),
            pltpu.VMEM((SECTIONS,) + field, f32),
            pltpu.VMEM((SECTIONS,) + field, f32),
            pltpu.VMEM((SECTIONS,) + field, f32),
            pltpu.VMEM((SECTIONS,) + field, f32),
            pltpu.VMEM((3,) + field, f32),
            pltpu.VMEM((3,) + field, f32),
            pltpu.VMEM((3,) + field, f32),
            pltpu.VMEM((3,) + field, f32),
            pltpu.VMEM((2,) + field, f32),
            pltpu.VMEM((3,) + field, f32),
            pltpu.VMEM((SECTIONS, SUB, ext_y), f32),
            pltpu.VMEM((SUB, ext_y), f32),
            pltpu.VMEM((2, ext_x, ext_x, SUB // ext_x, SUB, ext_y), f32),
            pltpu.VMEM((SUB, ext_y), f32),
            pltpu.VMEM((rounds, 2, 3, SUB, ext_y), f32),
            pltpu.VMEM((rounds, 2, 3, SUB, ext_y), f32),
            pltpu.VMEM((rounds, 2, packs, 3, SUB, ext_y), f32),
            pltpu.VMEM((rounds, 2, packs, 3, SUB, ext_y), f32),
            pltpu.VMEM((2, 1, ext_y), f32),
            pltpu.VMEM((slots, 1, ext_y), f32),
            pltpu.SemaphoreType.DMA((rounds, 6)),
            pltpu.SemaphoreType.DMA((rounds, 6)),
            pltpu.SemaphoreType.DMA((slots,)),
            pltpu.SemaphoreType.DMA((slots,)),
        ],
        compiler_params=pltpu.CompilerParams(
            collective_id=0, has_side_effects=True, vmem_limit_bytes=60 * 1024 * 1024
        ),
    )(
        depth0.reshape(field),
        momentum0.reshape((2,) + field),
        obs_weight.reshape(field),
        wet_mask.reshape(wet_mask.shape[1:]),
        zone_id,
        manning,
    )
    anywhere = pl.BlockSpec(memory_space=pl.ANY)
    adjoint, grad = pl.pallas_call(
        hand_over,
        out_shape=(
            jax.ShapeDtypeStruct(adjoint.shape, f32),
            jax.ShapeDtypeStruct(grad.shape, f32),
        ),
        in_specs=[anywhere] * 2,
        out_specs=(anywhere, anywhere),
        scratch_shapes=[
            pltpu.VMEM(adjoint.shape, f32),
            pltpu.VMEM(grad.shape, f32),
            pltpu.SemaphoreType.DMA((8,)),
        ],
    )(adjoint, grad)
    return adjoint.reshape((1, 3, NP, NP, ext_x, ext_y)), grad.reshape((ZONES,))


def solution(mesh):
    in_specs = (
        P(("basin", "ev"), None, None, "tx", "ty"),
        P(("basin", "ev"), None, None, None, "tx", "ty"),
        P(("basin", "ev"), None, None, "tx", "ty"),
        P(("basin", "ev"), None, "tx", "ty"),
        P(("basin", "tx"), "ty"),
        P("basin"),
    )
    out_specs = (P(("basin", "ev"), None, None, None, "tx", "ty"), P("basin"))
    return jax.shard_map(
        functools.partial(local, dict(mesh.shape)),
        mesh=mesh, in_specs=in_specs, out_specs=out_specs, check_vma=False,
    )
```
